256 devices in a mesh: inst: 32 (over z, x), head: 8 (over y, core).
Axes of the slice: x: 4, y: 4, z: 8, core: 2. Of those that a mesh axis runs over, the one named last changes fastest.
Arguments:
- latent_cache: bfloat16 [1024, 128, 512], P('inst'), may hold values from -6 to 6
- rope_cache: bfloat16 [1024, 128, 64], P('inst'), may hold values from -6 to 6
- query_nope: bfloat16 [2, 8, 128, 128], P(None, None, 'head'), may hold values from -6 to 6
- query_rope: bfloat16 [2, 8, 128, 64], P(None, None, 'head'), may hold values from -384 to 384
- key_absorb: bfloat16 [128, 128, 512], P('head'), may hold values from -0.5 to 0.5
- value_up_weight: bfloat16 [128, 512, 128], P('head'), may hold values from -0.25 to 0.25
- block_request: int32 [1024], replicated, may hold values from -1 to 7, as said below
- block_index: int32 [1024], replicated, may hold values from 0 to 79, as said below
- request_length: int32 [8], replicated, may hold values from 1 to 10240, as said below
- move_plan: int32 [1024], replicated, may hold values from -1 to 1023, as said below
Outputs:
- attention: float32 [2, 8, 128, 128], P(None, None, 'head')
- moved_latent: bfloat16 [1024, 128, 512], P('inst')
- moved_rope: bfloat16 [1024, 128, 64], P('inst')
The draws below stay inside these ranges and needn't reach their ends.
Inputs may be any that keep to these rules, and one draw needn't show every extreme that they name: `block_request`: half of the instances retire: each block they hold has a move_plan entry; an instance's blocks fill its first slots; each request's blocks are one run of at least one block in the order of instances and slots. `block_index`: counts blocks from 0 along a request's run; 0 for an empty slot. `request_length`: A request with c blocks has from 128 * (c - 1) + 1 to 128 * c tokens. `move_plan`: targets are empty slots of staying instances, no two alike; at most 2 blocks go from one instance to one other and some pair reaches it; at some staying instance its own and its arriving blocks fill all 32 slots.
All inputs are finite; a program needn't handle non-finite values.
Results may differ from the reference program's by a relative error of at most 0.007.
Values may be sent and summed in bfloat16 or wider, within the bound.
A program may use at most 128 MiB of HBM per device.

```python
import jax
import jax.numpy as jnp
from jax import lax

KVR = 512
ROPE = 64
NOPE = 128
VDIM = 128
HEADS = 128
BLOCK = 128
STEPS = 2
BLK_DEV = 32
REQS = 8
BLOCKS = 1024


def layout(key):
    instances = BLOCKS // BLK_DEV
    staying_count = instances // 2
    keys = jax.random.split(key, 5)
    order = jax.random.permutation(keys[0], instances).astype(jnp.int32)
    keepers = order[:staying_count]
    leavers = order[staying_count:]
    leaver_load = jax.random.randint(keys[1], (staying_count,), BLK_DEV // 2, BLK_DEV + 1).astype(jnp.int32)
    leaver_load = leaver_load.at[0].set(BLK_DEV)
    column = jnp.arange(BLK_DEV, dtype=jnp.int32)
    sender_ids = jnp.arange(staying_count, dtype=jnp.int32)
    target = (sender_ids[:, None] + column[None, :]) % staying_count
    live = column[None, :] < leaver_load[:, None]
    flat_target = target.reshape(-1)
    hits = ((flat_target[:, None] == sender_ids[None, :]) & live.reshape(-1)[:, None]).astype(jnp.int32)
    received = jnp.sum(hits, axis=0)
    keeper_load = (BLK_DEV - received).astype(jnp.int32)
    incoming_order = jnp.sum((jnp.cumsum(hits, axis=0) - 1) * hits, axis=1)
    landing = keepers[flat_target] * BLK_DEV + keeper_load[flat_target] + incoming_order
    sources = (leavers[:, None] * BLK_DEV + column[None, :]).reshape(-1)
    move_plan = jnp.full((BLOCKS,), -1, jnp.int32).at[sources].set(jnp.where(live.reshape(-1), landing, -1).astype(jnp.int32))
    load = jnp.zeros((instances,), jnp.int32).at[keepers].set(keeper_load).at[leavers].set(leaver_load)
    slot_ids = jnp.arange(BLOCKS, dtype=jnp.int32)
    occupied = slot_ids % BLK_DEV < load[slot_ids // BLK_DEV]
    live_rank = jnp.cumsum(occupied.astype(jnp.int32)) - 1
    live_total = BLOCKS // 2
    spacing = BLOCKS // (2 * REQS)
    reach = spacing // 4
    half_reach = reach // 2
    jitter = jax.random.randint(keys[3], (REQS - 1,), -half_reach, half_reach + 1).astype(jnp.int32)
    jitter = jitter.at[0].set(reach)
    inner = jnp.arange(1, REQS, dtype=jnp.int32) * spacing + jitter
    starts = jnp.concatenate([jnp.zeros((1,), jnp.int32), inner, jnp.full((1,), live_total, jnp.int32)])
    request_of = jnp.sum((live_rank[:, None] >= inner[None, :]).astype(jnp.int32), axis=1)
    block_request = jnp.where(occupied, request_of, -1).astype(jnp.int32)
    block_index = jnp.where(occupied, live_rank - starts[request_of], 0).astype(jnp.int32)
    counts_per = starts[1:] - starts[:-1]
    trimmed = jax.random.randint(keys[4], (REQS,), 0, BLOCK).astype(jnp.int32).at[0].set(0)
    lengths = (counts_per * BLOCK - trimmed).astype(jnp.int32)
    return (block_request, block_index, lengths, move_plan)


def draw_block_request(key, part):
    return layout(key)[0]


def draw_block_index(key, part):
    return layout(key)[1]


def draw_request_length(key, part):
    return layout(key)[2]


def draw_move_plan(key, part):
    return layout(key)[3]


def draw_query_rope(key, part):
    key = jax.random.fold_in(key, 11)
    base_key = jax.random.fold_in(key, 0)
    base = jnp.clip(jax.random.normal(base_key, (STEPS, REQS, HEADS, ROPE), jnp.float32), -6.0, 6.0)
    return (base * 2.0).astype(jnp.bfloat16)


def levels(rng, shape, pieces, least, top_value):
    def one(dim, parts):
        heights = jax.random.uniform(jax.random.fold_in(jax.random.fold_in(rng, 6), dim), (parts,), jnp.float32, least / len(pieces), top_value / len(pieces))
        return jnp.repeat(jnp.exp(heights), shape[dim] // parts).reshape((-1,) + (1,) * (len(shape) - dim - 1))

    gain = one(*pieces[0])
    for cut in pieces[1:]:
        gain = gain * one(*cut)
    return gain


def normal_values(stream_key, shape, scale, bound, pieces=(), kind=jnp.bfloat16):
    loudness = levels(stream_key, shape, pieces, -0.22, 0.18) if pieces else 1.0
    array = jax.random.normal(stream_key, shape, jnp.float32) * scale * loudness
    return jnp.minimum(jnp.maximum(array, -bound), bound).astype(kind)


def setup_inputs(seed: int = 0) -> dict:
    key_list = jax.random.split(jax.random.key(seed), 11)
    return {
        "latent_cache": normal_values(key_list[0], (BLOCKS, BLOCK, KVR), 1.0, 6.0, ((0, 32),)),
        "rope_cache": normal_values(key_list[1], (BLOCKS, BLOCK, ROPE), 1.0, 6.0, ((0, 32),)),
        "query_nope": normal_values(key_list[2], (STEPS, REQS, HEADS, NOPE), 1.0, 6.0, ((2, 8),)),
        "query_rope": draw_query_rope(jax.random.fold_in(key_list[10], 71), 0),
        "key_absorb": normal_values(key_list[4], (HEADS, NOPE, KVR), NOPE ** -0.5, 0.5, ((0, 8),)),
        "value_up_weight": normal_values(key_list[5], (HEADS, KVR, VDIM), KVR ** -0.5, 0.25, ((0, 8),)),
        "block_request": draw_block_request(jax.random.fold_in(key_list[10], 71), 0),
        "block_index": draw_block_index(jax.random.fold_in(key_list[10], 71), 0),
        "request_length": draw_request_length(jax.random.fold_in(key_list[10], 71), 0),
        "move_plan": draw_move_plan(jax.random.fold_in(key_list[10], 71), 0),
    }


def token_mask(block_request, block_index, request_length):
    within = jnp.arange(BLOCK, dtype=jnp.int32)
    token_holder = jnp.repeat(block_request, BLOCK)
    token_place = (block_index[:, None] * BLOCK + within[None, :]).reshape(-1)
    wanted = jnp.arange(REQS, dtype=jnp.int32)
    return (token_holder[None, :] == wanted[:, None]) & (token_place[None, :] < request_length[:, None])


def reference(latent_cache, rope_cache, query_nope, query_rope, key_absorb, value_up_weight, block_request, block_index, request_length, move_plan):
    latent_rows = latent_cache.reshape(BLOCKS * BLOCK, KVR)
    rope_rows = rope_cache.reshape(BLOCKS * BLOCK, ROPE)
    visible = token_mask(block_request, block_index, request_length)
    scaling = (NOPE + ROPE) ** -0.5
    contract = (((1,), (1,)), ((), ()))

    def one_head(inputs):
        latent_query, rope_query, value_weight = inputs
        scores = (lax.dot_general(latent_query, latent_rows, contract, preferred_element_type=jnp.float32)
                  + lax.dot_general(rope_query, rope_rows, contract, preferred_element_type=jnp.float32)) * scaling
        scores = jnp.where(visible, scores, -1e30)
        row_peak = jnp.max(scores, axis=1, keepdims=True)
        weights = jnp.where(visible, jnp.exp(scores - row_peak), 0.0)
        weight_sum = jnp.sum(weights, axis=1, keepdims=True)
        summed = jnp.dot(weights.astype(jnp.bfloat16), latent_rows, preferred_element_type=jnp.float32)
        weighted_latent = (summed / weight_sum).astype(jnp.bfloat16)
        return jnp.dot(weighted_latent, value_weight, preferred_element_type=jnp.float32)

    results = []
    for step_index in range(STEPS):
        absorbed = jnp.einsum("rhn,hnk->rhk", query_nope[step_index].astype(jnp.float32),
                              key_absorb.astype(jnp.float32)).astype(jnp.bfloat16)
        per_head = lax.map(one_head, (absorbed.transpose(1, 0, 2), query_rope[step_index].transpose(1, 0, 2), value_up_weight))
        results.append(per_head.transpose(1, 0, 2))
    attention = jnp.stack(results)

    slot_ids = jnp.arange(BLOCKS, dtype=jnp.int32)
    staying = (block_request >= 0) & (move_plan < 0)
    landing = jnp.where(move_plan >= 0, move_plan, jnp.where(staying, slot_ids, BLOCKS)).astype(jnp.int32)
    moved_latent = jnp.zeros_like(latent_cache).at[landing].set(latent_cache, mode="drop")
    moved_rope = jnp.zeros_like(rope_cache).at[landing].set(rope_cache, mode="drop")
    return attention, moved_latent, moved_rope
```

```python
import functools

import jax
import jax.numpy as jnp
from jax import lax
from jax.experimental import pallas as pl
from jax.experimental.pallas import tpu as pltpu
from jax.sharding import PartitionSpec as P

MESH = pl.DeviceIdType.MESH
HIDDEN = -1e30
FLOOR = -1e29
TILE = 128
ROWS = 16
LANE_TILES = ((0, 1), (2, 3))
ROPE_CHUNK = 1
NEG = -1


def kernel(
    lat_hbm,
    rope_hbm,
    nope_hbm,
    qrope_hbm,
    absorb_hbm,
    value_hbm,
    owner_hbm,
    index_hbm,
    length_hbm,
    plan_hbm,
    out_att,
    out_lat,
    out_rope,
    lat_vm,
    rope_vm,
    nope_vm,
    qrope_vm,
    absorb_vm,
    value_vm,
    plan_vm,
    owner_sm,
    index_sm,
    length_sm,
    table_vm,
    table_sm,
    share,
    rope_share,
    landed,
    landed_rope,
    rope_got,
    query,
    scores,
    att_send,
    att_got,
    att_all,
    send0,
    send1,
    got0,
    got1,
    in_sem,
    a2a_send,
    a2a_recv,
    att_sem,
    own_sem,
    ag_send,
    ag_recv,
):
    insts = lax.axis_size("inst")
    me = lax.axis_index("inst")
    head = lax.axis_index("head")
    core = lax.rem(head, 2)
    y = head // 2
    up = lax.rem(y + 1, 4)
    down = lax.rem(y + 3, 4)
    far = lax.rem(y + 2, 4)
    other = 1 - core
    slots = lat_vm.shape[0]
    sends, gots = (send0, send1), (got0, got1)
    parts = len(LANE_TILES)

    def fetch(k, source, target):
        copy = pltpu.make_async_copy(source, target, in_sem.at[k])
        copy.start()
        return copy

    rows = pl.ds(pl.multiple_of(head * ROWS, ROWS), ROWS)
    get_plan = fetch(0, plan_hbm, plan_vm)
    get_share = fetch(1, lat_hbm.at[:, rows, :], share)
    get_rope = fetch(2, rope_hbm, rope_vm)
    get_owner = fetch(3, owner_hbm, owner_sm)
    get_index = fetch(4, index_hbm, index_sm)
    get_length = fetch(5, length_hbm, length_sm)
    get_nope = fetch(6, nope_hbm, nope_vm)
    get_absorb = fetch(7, absorb_hbm, absorb_vm)
    get_qrope = fetch(8, qrope_hbm, qrope_vm)
    get_lat = fetch(9, lat_hbm, lat_vm)
    get_value = fetch(10, value_hbm, value_vm)

    barrier = pltpu.get_barrier_semaphore()

    def greet(k, carry):
        pl.semaphore_signal(
            barrier,
            inc=1,
            device_id={"inst": lax.rem(me + k, insts)},
            device_id_type=MESH,
        )
        return carry

    lax.fori_loop(1, insts, greet, 0)
    mates = (y * 2 + other, up * 2 + core, down * 2 + core)
    for mate in mates:
        pl.semaphore_signal(barrier, inc=1, device_id={"head": mate}, device_id_type=MESH)

    get_plan.wait()
    plan = plan_vm[...]
    lane = lax.broadcasted_iota(jnp.int32, (8, TILE), 1)
    row = lax.broadcasted_iota(jnp.int32, (8, TILE), 0)
    per_row = TILE // slots
    group = lane // slots
    within = lane - group * slots
    seen = jnp.where((plan >> 5) == me, 1, 0)
    for d in (1, 2, 4, 8, 16):
        seen = jnp.maximum(seen, jnp.where(within >= d, pltpu.roll(seen, d, 1), 0))
    rank = jnp.where(within >= 1, pltpu.roll(seen, 1, 1), 0)
    code = (row * per_row + group) * 2 + rank
    column = lax.broadcasted_iota(jnp.int32, (slots, TILE), 0)
    lanes = lax.broadcasted_iota(jnp.int32, (slots, TILE), 1)
    hit = jnp.full((slots, TILE), NEG, jnp.int32)
    for r in range(8):
        wanted = jnp.broadcast_to(plan[r : r + 1, :], (slots, TILE)) == me * slots + column
        hit = jnp.maximum(
            hit, jnp.where(wanted, jnp.broadcast_to(code[r : r + 1, :], (slots, TILE)), NEG)
        )
    land = jnp.max(hit, axis=1, keepdims=True)
    mine = plan_vm[pl.ds(me // per_row, 1), :]
    own_lane = lax.rem(me, per_row) * slots + column
    own = jnp.max(
        jnp.where(lanes == own_lane, jnp.broadcast_to(mine, (slots, TILE)), NEG),
        axis=1,
        keepdims=True,
    )
    mine = jnp.where(group[:1] == lax.rem(me, per_row), mine >> 5, NEG)
    goes = jnp.broadcast_to(mine, (slots, TILE)) == column
    place = lanes - lanes // slots * slots
    first = jnp.min(jnp.where(goes, place, slots), axis=1, keepdims=True)
    last = jnp.max(jnp.where(goes, place, 0), axis=1, keepdims=True)
    first = jnp.where(first >= slots, 0, first)
    table_vm[...] = jnp.where(
        lanes == 0,
        jnp.broadcast_to(first, (slots, TILE)),
        jnp.where(
            lanes == 1,
            jnp.broadcast_to(last, (slots, TILE)),
            jnp.where(
                lanes == 2,
                jnp.broadcast_to(land, (slots, TILE)),
                jnp.broadcast_to(own, (slots, TILE)),
            ),
        ),
    )
    get_table = fetch(11, table_vm, table_sm)

    get_rope.wait()
    half = pl.ds(pl.multiple_of(y * ROWS, ROWS), ROWS)

    def cut_rope(t, carry):
        piece = rope_vm[t, half, :].astype(jnp.float32)
        rope_share[t] = jnp.where(core == 0, piece[:8], piece[8:])
        return carry

    lax.fori_loop(0, slots, cut_rope, 0, unroll=4)
    get_share.wait()
    get_table.wait()
    get_owner.wait()
    get_index.wait()
    get_length.wait()

    for part in range(parts):
        tiles = LANE_TILES[part]
        count = len(tiles)
        buffer = sends[part]

        def pack(j, carry, tiles=tiles, count=count, buffer=buffer, part=part):
            picks = (table_sm[j, 0], table_sm[j, 1])
            for seat in range(2):
                for n, tile in enumerate(tiles):
                    buffer[j, seat * count + n] = share[
                        picks[seat], :, tile * TILE : (tile + 1) * TILE
                    ]
            if part == ROPE_CHUNK:
                buffer[j, 2 * count] = jnp.concatenate(
                    [rope_share[picks[0]], rope_share[picks[1]]], axis=0
                ).astype(jnp.bfloat16)
            return carry

        lax.fori_loop(0, insts, pack, 0, unroll=4)
        if part == 0:
            pl.semaphore_wait(barrier, insts - 1 + len(mates))

        def ship(k, carry, part=part, buffer=buffer):
            peer = lax.rem(me + k, insts)
            pltpu.make_async_remote_copy(
                src_ref=buffer.at[peer],
                dst_ref=gots[part].at[me],
                send_sem=a2a_send.at[part],
                recv_sem=a2a_recv.at[part],
                device_id={"inst": peer},
                device_id_type=MESH,
            ).start()
            return carry

        lax.fori_loop(1, insts, ship, 0)

    heads = 16
    queries = nope_vm.shape[0]
    row_head = lax.rem(lax.broadcasted_iota(jnp.int32, (queries, 1), 0), heads)
    row_request = lax.rem(lax.broadcasted_iota(jnp.int32, (queries, 1), 0) // heads, 8)
    get_nope.wait()
    get_absorb.wait()
    width = lat_vm.shape[2]

    def absorb(h, total):
        part_query = jnp.where(row_head == h, nope_vm[...], jnp.zeros((), jnp.bfloat16))
        return total + jnp.dot(part_query, absorb_vm[h], preferred_element_type=jnp.float32)

    absorbed = lax.fori_loop(0, heads, absorb, jnp.zeros((queries, width), jnp.float32))
    query[...] = absorbed.astype(jnp.bfloat16)
    get_qrope.wait()
    get_lat.wait()
    scale = 192.0**-0.5
    pair = 2 * TILE
    lane_row = lax.broadcasted_iota(jnp.int32, (1, TILE), 1)

    def score(i, peak):
        block = lat_vm[pl.ds(2 * i, 2)].reshape(pair, width)
        raw = lax.dot_general(
            query[...], block, (((1,), (1,)), ((), ())), preferred_element_type=jnp.float32
        )
        turned = []
        holders = []
        for b in range(2):
            turned.append(
                jnp.dot(qrope_vm[...], rope_vm[2 * i + b], preferred_element_type=jnp.float32)
            )
            g = lax.rem(me, per_row) * slots + 2 * i + b
            owner = owner_sm[me // per_row, g]
            left = length_sm[jnp.maximum(owner, 0)] - index_sm[me // per_row, g] * TILE
            holders.append(jnp.where(lane_row < left, owner, NEG))
        raw = (raw + jnp.concatenate(turned, axis=1)) * scale
        raw = jnp.where(jnp.concatenate(holders, axis=1) == row_request, raw, HIDDEN)
        scores[i] = raw
        return jnp.maximum(peak, raw)

    peak = lax.fori_loop(
        0, slots // 2, score, jnp.full((queries, pair), FLOOR, jnp.float32)
    )
    peak = jnp.max(peak, axis=1, keepdims=True)

    def weigh(i, carry):
        total, summed = carry
        weights = jnp.exp(scores[i] - peak)
        block = lat_vm[pl.ds(2 * i, 2)].reshape(pair, width)
        summed = summed + jnp.dot(
            weights.astype(jnp.bfloat16), block, preferred_element_type=jnp.float32
        )
        return total + weights, summed

    total, summed = lax.fori_loop(
        0,
        slots // 2,
        weigh,
        (jnp.zeros((queries, pair), jnp.float32), jnp.zeros((queries, width), jnp.float32)),
    )
    total = jnp.sum(total, axis=1, keepdims=True)
    query[...] = summed.astype(jnp.bfloat16)
    get_value.wait()

    def project(n, result):
        both = jnp.concatenate([value_vm[2 * n], value_vm[2 * n + 1]], axis=1)
        got = jnp.dot(query[...], both, preferred_element_type=jnp.float32)
        result = jnp.where(row_head == 2 * n, got[:, :TILE], result)
        return jnp.where(row_head == 2 * n + 1, got[:, TILE:], result)

    projected = lax.fori_loop(
        0, heads // 2, project, jnp.zeros((queries, TILE), jnp.float32)
    )
    wide = lax.broadcasted_iota(jnp.int32, (queries, TILE), 1)
    stats = jnp.where(
        wide < TILE // 2,
        jnp.broadcast_to(peak, (queries, TILE)),
        jnp.broadcast_to(total, (queries, TILE)),
    )
    att_send[:, 0] = projected.reshape(insts, 8, TILE)
    att_send[:, 1] = stats.reshape(insts, 8, TILE)
    att_got[me] = att_send[me]

    def ship_partial(k, carry):
        peer = lax.rem(me + k, insts)
        pltpu.make_async_remote_copy(
            src_ref=att_send.at[peer],
            dst_ref=att_got.at[me],
            send_sem=att_sem.at[0],
            recv_sem=att_sem.at[1],
            device_id={"inst": peer},
            device_id_type=MESH,
        ).start()
        return carry

    lax.fori_loop(1, insts, ship_partial, 0)

    def wait_all(buffer, sem):
        whole = buffer.at[pl.ds(0, insts - 1)]
        pltpu.make_async_copy(whole, whole, sem).wait()

    def region(unit, h, which):
        n = slots if unit < parts else slots // 2
        span = {
            None: pl.ds(0, n),
            0: pl.ds(0, n // 2),
            1: pl.ds(n // 2, n // 2),
        }[which]
        if unit < parts:
            tiles = LANE_TILES[unit]
            return out_lat.at[
                span,
                pl.ds(pl.multiple_of(h * ROWS, ROWS), ROWS),
                pl.ds(tiles[0] * TILE, len(tiles) * TILE),
            ]
        return out_rope.at[h, span]

    def own_region(unit):
        if unit < parts:
            tiles = LANE_TILES[unit]
            return landed.at[:, :, pl.ds(tiles[0] * TILE, len(tiles) * TILE)]
        return landed_rope

    started = []

    def send(unit, k, source, h, which, mate):
        copy = pltpu.make_async_remote_copy(
            src_ref=source,
            dst_ref=region(unit, h, which),
            send_sem=ag_send.at[unit, k],
            recv_sem=ag_recv.at[unit, k],
            device_id={"head": mate},
            device_id_type=MESH,
        )
        copy.start()
        started.append(copy)

    def arrived(unit, k, h, which):
        here = region(unit, h, which)
        pltpu.make_async_copy(here, here, ag_recv.at[unit, k]).wait()

    side, above, below = mates
    h_up, h_down, h_far = up * 2 + core, down * 2 + core, far * 2 + core
    o_up, o_down, o_far = up * 2 + other, down * 2 + other, far * 2 + other
    keeping = []

    def place_part(part):
        tiles = LANE_TILES[part]
        count = len(tiles)
        buffer = gots[part]
        wait_all(buffer, a2a_recv.at[part])

        def put(t, carry):
            where = table_sm[t, 2]
            g = lax.rem(me, per_row) * slots + t
            keep = (owner_sm[me // per_row, g] >= 0) & (table_sm[t, 3] < 0)
            spot = jnp.maximum(where, 0)
            source, seat = spot // 2, lax.rem(spot, 2)
            for n, tile in enumerate(tiles):
                span = slice(tile * TILE, (tile + 1) * TILE)
                moved = buffer[source, seat * count + n]
                kept = share[t, :, span]
                zero = jnp.zeros_like(moved)
                landed[t, :, span] = jnp.where(
                    keep, kept, jnp.where(where >= 0, moved, zero)
                )
            if part == ROPE_CHUNK:
                pieces = buffer[source, 2 * count].astype(jnp.float32)
                moved = jnp.where(seat == 0, pieces[:8], pieces[8:])
                zero = jnp.zeros_like(moved)
                rope_got[t] = jnp.where(
                    keep, rope_share[t], jnp.where(where >= 0, moved, zero)
                )
            return carry

        lax.fori_loop(0, slots, put, 0, unroll=4)
        units = [part]
        if part == ROPE_CHUNK:
            landed_rope[...] = (
                rope_got[...].reshape(slots // 2, ROWS, TILE).astype(jnp.bfloat16)
            )
            units.append(parts)
        for unit in units:
            source = own_region(unit)
            copy = pltpu.make_async_copy(source, region(unit, head, None), own_sem.at[unit])
            copy.start()
            keeping.append(copy)
            send(unit, 1, source, head, None, above)
            send(unit, 2, source, head, None, below)
            send(unit, 0, source, head, None, side)

    def relay(unit):
        arrived(unit, 1, h_down, None)
        send(unit, 5, region(unit, h_down, 0), h_down, 0, above)
        send(unit, 3, region(unit, h_down, None), h_down, None, side)
        arrived(unit, 2, h_up, None)
        send(unit, 6, region(unit, h_up, 1), h_up, 1, below)
        send(unit, 4, region(unit, h_up, None), h_up, None, side)

    def finish(unit):
        arrived(unit, 5, h_far, 0)
        send(unit, 7, region(unit, h_far, 0), h_far, 0, side)
        arrived(unit, 6, h_far, 1)
        send(unit, 8, region(unit, h_far, 1), h_far, 1, side)

    def combine():
        wait_all(att_got, att_sem.at[1])
        got = att_got[...]
        partial, stat = got[:, 0], got[:, 1]
        peaks, totals = stat[:, :, :1], stat[:, :, TILE // 2 : TILE // 2 + 1]
        top = jnp.max(peaks, axis=0, keepdims=True)
        weight = jnp.exp(peaks - top)
        above_line = jnp.sum(partial * weight, axis=0)
        below_line = jnp.sum(totals * weight, axis=0)
        att_all[me] = above_line / below_line

        def ship_result(k, carry):
            pltpu.make_async_remote_copy(
                src_ref=att_all.at[me],
                dst_ref=att_all.at[me],
                send_sem=att_sem.at[2],
                recv_sem=att_sem.at[3],
                device_id={"inst": lax.rem(me + k, insts)},
                device_id_type=MESH,
            ).start()
            return carry

        lax.fori_loop(1, insts, ship_result, 0)

    place_part(0)
    combine()
    place_part(1)
    relay(0)
    relay(1)
    relay(2)
    finish(0)
    finish(1)
    finish(2)

    wait_all(att_all, att_sem.at[3])
    out_att[...] = att_all[...].reshape(queries, TILE)
    for unit in range(parts + 1):
        arrived(unit, 0, y * 2 + other, None)
        arrived(unit, 3, o_down, None)
        arrived(unit, 4, o_up, None)
        arrived(unit, 7, o_far, 0)
        arrived(unit, 8, o_far, 1)
    for copy in keeping:
        copy.wait()
    for copy in started:
        copy.wait_send()
    for part in range(parts):
        wait_all(sends[part], a2a_send.at[part])
    wait_all(att_send, att_sem.at[0])
    wait_all(att_all, att_sem.at[2])


def shards(
    latent_cache,
    rope_cache,
    query_nope,
    query_rope,
    key_absorb,
    value_up_weight,
    block_request,
    block_index,
    request_length,
    move_plan,
):
    slots, block, width = latent_cache.shape
    rope_width = rope_cache.shape[2]
    steps, requests, heads, nope_width = query_nope.shape
    queries = steps * requests * heads
    insts = lax.axis_size("inst")
    heads_axis = lax.axis_size("head")
    bf16, f32, i32 = jnp.bfloat16, jnp.float32, jnp.int32
    tiles = [
        2 * len(LANE_TILES[p]) + (1 if p == ROPE_CHUNK else 0) for p in range(len(LANE_TILES))
    ]
    units = len(LANE_TILES) + 1
    anywhere = pl.BlockSpec(memory_space=pl.ANY)
    attention, moved, rope = pl.pallas_call(
        kernel,
        out_shape=(
            jax.ShapeDtypeStruct((queries, TILE), f32),
            jax.ShapeDtypeStruct(latent_cache.shape, bf16),
            jax.ShapeDtypeStruct((heads_axis, slots // 2, ROWS, TILE), bf16),
        ),
        in_specs=[anywhere] * 10,
        out_specs=(pl.BlockSpec(memory_space=pltpu.VMEM), anywhere, anywhere),
        scratch_shapes=[
            pltpu.VMEM((slots, block, width), bf16),
            pltpu.VMEM((slots, rope_width, block), bf16),
            pltpu.VMEM((queries, nope_width), bf16),
            pltpu.VMEM((queries, rope_width), bf16),
            pltpu.VMEM(key_absorb.shape, bf16),
            pltpu.VMEM(value_up_weight.shape, bf16),
            pltpu.VMEM((8, TILE), i32),
            pltpu.SMEM((8, TILE), i32),
            pltpu.SMEM((8, TILE), i32),
            pltpu.SMEM((8,), i32),
            pltpu.VMEM((slots, TILE), i32),
            pltpu.SMEM((slots, TILE), i32),
            pltpu.VMEM((slots, ROWS, width), bf16),
            pltpu.VMEM((slots, 8, TILE), f32),
            pltpu.VMEM((slots, ROWS, width), bf16),
            pltpu.VMEM((slots // 2, ROWS, TILE), bf16),
            pltpu.VMEM((slots, 8, TILE), f32),
            pltpu.VMEM((queries, width), bf16),
            pltpu.VMEM((slots // 2, queries, 2 * TILE), f32),
            pltpu.VMEM((insts, 2, 8, TILE), f32),
            pltpu.VMEM((insts, 2, 8, TILE), f32),
            pltpu.VMEM((insts, 8, TILE), f32),
        ]
        + [pltpu.VMEM((insts, n, ROWS, TILE), bf16) for n in tiles]
        + [pltpu.VMEM((insts, n, ROWS, TILE), bf16) for n in tiles]
        + [
            pltpu.SemaphoreType.DMA((12,)),
            pltpu.SemaphoreType.DMA((len(tiles),)),
            pltpu.SemaphoreType.DMA((len(tiles),)),
            pltpu.SemaphoreType.DMA((4,)),
            pltpu.SemaphoreType.DMA((units,)),
            pltpu.SemaphoreType.DMA((units, 9)),
            pltpu.SemaphoreType.DMA((units, 9)),
        ],
        compiler_params=pltpu.CompilerParams(
            collective_id=0, has_side_effects=True, vmem_limit_bytes=56 * 2**20
        ),
        name="decode_and_move",
    )(
        latent_cache,
        rope_cache.swapaxes(1, 2),
        query_nope.reshape(queries, nope_width),
        query_rope.reshape(queries, rope_width),
        key_absorb,
        value_up_weight,
        block_request.reshape(8, TILE),
        block_index.reshape(8, TILE),
        request_length,
        move_plan.reshape(8, TILE),
    )
    rope = rope.reshape(heads_axis, slots, 8, TILE).swapaxes(0, 1)
    rope = rope.reshape(slots, rope_width, block).swapaxes(1, 2)
    return attention.reshape(steps, requests, heads, TILE), moved, rope


def solution(mesh):
    return jax.shard_map(
        shards,
        mesh=mesh,
        in_specs=(
            P("inst", None, None),
            P("inst", None, None),
            P(None, None, "head", None),
            P(None, None, "head", None),
            P("head", None, None),
            P("head", None, None),
            P(),
            P(),
            P(),
            P(),
        ),
        out_specs=(P(None, None, "head", None), P("inst", None, None), P("inst", None, None)),
        check_vma=False,
    )
```

```python
import functools

import jax
import jax.numpy as jnp
from jax import lax
from jax.experimental import pallas as pl
from jax.experimental.pallas import tpu as pltpu
from jax.sharding import PartitionSpec as P

MESH = pl.DeviceIdType.MESH
HIDDEN = -1e30
FLOOR = -1e29
TILE = 128
ROWS = 16
LANE_TILES = ((0,), (1,), (2,), (3,))
ROPE_CHUNK = 0
Z, X = 8, 4
NEG = -1


def kernel(
    lat_hbm,
    rope_hbm,
    nope_hbm,
    qrope_hbm,
    absorb_hbm,
    value_hbm,
    owner_hbm,
    index_hbm,
    length_hbm,
    plan_hbm,
    out_att,
    out_lat,
    out_rope,
    lat_vm,
    rope_vm,
    nope_vm,
    qrope_vm,
    absorb_vm,
    value_vm,
    plan_vm,
    owner_sm,
    index_sm,
    length_sm,
    table_vm,
    table_sm,
    share,
    rope_share,
    rope_got,
    query,
    scores,
    x_send,
    x_got,
    z_send,
    z_got,
    z_all,
    x_all,
    *rest,

):
    parts = len(LANE_TILES)
    sends, gots = rest[:parts], rest[parts : 2 * parts]
    in_sem, a2a_send, a2a_recv, att_sem, ag_send, ag_recv = rest[2 * parts :]
    insts = lax.axis_size("inst")
    me = lax.axis_index("inst")
    head = lax.axis_index("head")
    core = lax.rem(head, 2)
    y = head // 2
    up = lax.rem(y + 1, 4)
    down = lax.rem(y + 3, 4)
    far = lax.rem(y + 2, 4)
    other = 1 - core
    slots = lat_vm.shape[0]
    z, x = me // X, lax.rem(me, X)

    def fetch(k, source, target):
        copy = pltpu.make_async_copy(source, target, in_sem.at[k])
        copy.start()
        return copy

    rows = pl.ds(pl.multiple_of(head * ROWS, ROWS), ROWS)
    get_plan = fetch(0, plan_hbm, plan_vm)
    get_share = fetch(1, lat_hbm.at[:, rows, :], share)
    get_rope = fetch(2, rope_hbm, rope_vm)
    get_owner = fetch(3, owner_hbm, owner_sm)
    get_index = fetch(4, index_hbm, index_sm)
    get_length = fetch(5, length_hbm, length_sm)
    get_nope = fetch(6, nope_hbm, nope_vm)
    get_absorb = fetch(7, absorb_hbm, absorb_vm)
    get_qrope = fetch(8, qrope_hbm, qrope_vm)
    get_lat = fetch(9, lat_hbm, lat_vm)
    get_value = fetch(10, value_hbm, value_vm)

    barrier = pltpu.get_barrier_semaphore()

    def greet(k, carry):
        pl.semaphore_signal(
            barrier,
            inc=1,
            device_id={"inst": lax.rem(me + k, insts)},
            device_id_type=MESH,
        )
        return carry

    lax.fori_loop(1, insts, greet, 0)
    mates = (y * 2 + other, up * 2 + core, down * 2 + core)
    for mate in mates:
        pl.semaphore_signal(barrier, inc=1, device_id={"head": mate}, device_id_type=MESH)

    get_plan.wait()
    plan = plan_vm[...]
    lane = lax.broadcasted_iota(jnp.int32, (8, TILE), 1)
    row = lax.broadcasted_iota(jnp.int32, (8, TILE), 0)
    per_row = TILE // slots
    group = lane // slots
    within = lane - group * slots
    seen = jnp.where((plan >> 5) == me, 1, 0)
    for d in (1, 2, 4, 8, 16):
        seen = jnp.maximum(seen, jnp.where(within >= d, pltpu.roll(seen, d, 1), 0))
    rank = jnp.where(within >= 1, pltpu.roll(seen, 1, 1), 0)
    code = (row * per_row + group) * 2 + rank
    column = lax.broadcasted_iota(jnp.int32, (slots, TILE), 0)
    lanes = lax.broadcasted_iota(jnp.int32, (slots, TILE), 1)
    hit = jnp.full((slots, TILE), NEG, jnp.int32)
    for r in range(8):
        wanted = jnp.broadcast_to(plan[r : r + 1, :], (slots, TILE)) == me * slots + column
        hit = jnp.maximum(
            hit, jnp.where(wanted, jnp.broadcast_to(code[r : r + 1, :], (slots, TILE)), NEG)
        )
    land = jnp.max(hit, axis=1, keepdims=True)
    mine = plan_vm[pl.ds(me // per_row, 1), :]
    own_lane = lax.rem(me, per_row) * slots + column
    own = jnp.max(
        jnp.where(lanes == own_lane, jnp.broadcast_to(mine, (slots, TILE)), NEG),
        axis=1,
        keepdims=True,
    )
    mine = jnp.where(group[:1] == lax.rem(me, per_row), mine >> 5, NEG)
    goes = jnp.broadcast_to(mine, (slots, TILE)) == column
    place = lanes - lanes // slots * slots
    first = jnp.min(jnp.where(goes, place, slots), axis=1, keepdims=True)
    last = jnp.max(jnp.where(goes, place, 0), axis=1, keepdims=True)
    first = jnp.where(first >= slots, 0, first)
    table_vm[...] = jnp.where(
        lanes == 0,
        jnp.broadcast_to(first, (slots, TILE)),
        jnp.where(
            lanes == 1,
            jnp.broadcast_to(last, (slots, TILE)),
            jnp.where(
                lanes == 2,
                jnp.broadcast_to(land, (slots, TILE)),
                jnp.broadcast_to(own, (slots, TILE)),
            ),
        ),
    )
    get_table = fetch(11, table_vm, table_sm)

    get_rope.wait()
    half = pl.ds(pl.multiple_of(y * ROWS, ROWS), ROWS)

    def cut_rope(t, carry):
        piece = rope_vm[t, half, :].astype(jnp.float32)
        rope_share[t] = jnp.where(core == 0, piece[:8], piece[8:])
        return carry

    lax.fori_loop(0, slots, cut_rope, 0, unroll=4)
    get_share.wait()
    get_table.wait()
    get_owner.wait()
    get_index.wait()
    get_length.wait()

    for part in range(parts):
        tiles = LANE_TILES[part]
        count = len(tiles)
        buffer = sends[part]

        def pack(j, carry, tiles=tiles, count=count, buffer=buffer, part=part):
            picks = (table_sm[j, 0], table_sm[j, 1])
            for seat in range(2):
                for n, tile in enumerate(tiles):
                    buffer[j, seat * count + n] = share[
                        picks[seat], :, tile * TILE : (tile + 1) * TILE
                    ]
            if part == ROPE_CHUNK:
                buffer[j, 2 * count] = jnp.concatenate(
                    [rope_share[picks[0]], rope_share[picks[1]]], axis=0
                ).astype(jnp.bfloat16)
            return carry

        lax.fori_loop(0, insts, pack, 0, unroll=4)
        if part == 0:
            pl.semaphore_wait(barrier, insts - 1 + len(mates))

        def ship(k, carry, part=part, buffer=buffer):
            peer = lax.rem(me + k, insts)
            pltpu.make_async_remote_copy(
                src_ref=buffer.at[peer],
                dst_ref=gots[part].at[me],
                send_sem=a2a_send.at[part],
                recv_sem=a2a_recv.at[part],
                device_id={"inst": peer},
                device_id_type=MESH,
            ).start()
            return carry

        lax.fori_loop(1, insts, ship, 0)

    def wait_all(buffer, sem):
        whole = buffer.at[pl.ds(0, buffer.shape[0] - 1)]
        pltpu.make_async_copy(whole, whole, sem).wait()

    def ship_part(source, target, k, peer):
        pltpu.make_async_remote_copy(
            src_ref=source,
            dst_ref=target,
            send_sem=att_sem.at[k, 0],
            recv_sem=att_sem.at[k, 1],
            device_id={"inst": peer},
            device_id_type=MESH,
        ).start()

    def merge(got):
        partial, stat = got[:, 0], got[:, 1]
        peaks, totals = stat[:, :, :1], stat[:, :, TILE // 2 : TILE // 2 + 1]
        top = jnp.max(peaks, axis=0, keepdims=True)
        weight = jnp.exp(peaks - top)
        return top[0], jnp.sum(partial * weight, axis=0), jnp.sum(totals * weight, axis=0)

    def region(unit, h, which):
        n = slots if unit < parts else slots // 2
        span = {
            None: pl.ds(0, n),
            0: pl.ds(0, n // 2),
            1: pl.ds(n // 2, n // 2),
        }[which]
        if unit < parts:
            tiles = LANE_TILES[unit]
            return out_lat.at[
                span,
                pl.ds(pl.multiple_of(h * ROWS, ROWS), ROWS),
                pl.ds(tiles[0] * TILE, len(tiles) * TILE),
            ]
        return out_rope.at[h, span]

    started = []

    def send(unit, k, source, h, which, mate):
        copy = pltpu.make_async_remote_copy(
            src_ref=source,
            dst_ref=region(unit, h, which),
            send_sem=ag_send.at[unit, k],
            recv_sem=ag_recv.at[unit, k],
            device_id={"head": mate},
            device_id_type=MESH,
        )
        copy.start()
        started.append(copy)

    def arrived(unit, k, h, which):
        here = region(unit, h, which)
        pltpu.make_async_copy(here, here, ag_recv.at[unit, k]).wait()

    side, above, below = mates
    h_up, h_down, h_far = up * 2 + core, down * 2 + core, far * 2 + core
    o_up, o_down, o_far = up * 2 + other, down * 2 + other, far * 2 + other
    extra = {part: [part] + [parts] * (part == ROPE_CHUNK) for part in range(parts)}

    def place(part):
        tiles = LANE_TILES[part]
        count = len(tiles)
        buffer = gots[part]
        wait_all(buffer, a2a_recv.at[part])

        def put(t, carry):
            where = table_sm[t, 2]
            g = lax.rem(me, per_row) * slots + t
            keep = (owner_sm[me // per_row, g] >= 0) & (table_sm[t, 3] < 0)
            spot = jnp.maximum(where, 0)
            source, seat = spot // 2, lax.rem(spot, 2)
            for n, tile in enumerate(tiles):
                span = slice(tile * TILE, (tile + 1) * TILE)
                moved = buffer[source, seat * count + n]
                kept = share[t, :, span]
                zero = jnp.zeros_like(moved)
                out_lat[t, rows, span] = jnp.where(
                    keep, kept, jnp.where(where >= 0, moved, zero)
                )
            if part == ROPE_CHUNK:
                pieces = buffer[source, 2 * count].astype(jnp.float32)
                moved = jnp.where(seat == 0, pieces[:8], pieces[8:])
                zero = jnp.zeros_like(moved)
                rope_got[t] = jnp.where(
                    keep, rope_share[t], jnp.where(where >= 0, moved, zero)
                )
            return carry

        lax.fori_loop(0, slots, put, 0, unroll=4)
        if part == ROPE_CHUNK:
            out_rope[head] = rope_got[...].reshape(slots // 2, ROWS, TILE).astype(jnp.bfloat16)
        for unit in extra[part]:
            source = region(unit, head, None)
            send(unit, 1, source, head, None, above)
            send(unit, 2, source, head, None, below)
            send(unit, 0, source, head, None, side)

    def relay(part):
        for unit in extra[part]:
            arrived(unit, 1, h_down, None)
            send(unit, 5, region(unit, h_down, 0), h_down, 0, above)
            send(unit, 3, region(unit, h_down, None), h_down, None, side)
            arrived(unit, 2, h_up, None)
            send(unit, 6, region(unit, h_up, 1), h_up, 1, below)
            send(unit, 4, region(unit, h_up, None), h_up, None, side)

    def finish(part):
        for unit in extra[part]:
            arrived(unit, 5, h_far, 0)
            send(unit, 7, region(unit, h_far, 0), h_far, 0, side)
            arrived(unit, 6, h_far, 1)
            send(unit, 8, region(unit, h_far, 1), h_far, 1, side)

    heads = 16
    queries = nope_vm.shape[0]
    row_head = lax.rem(lax.broadcasted_iota(jnp.int32, (queries, 1), 0), heads)
    row_request = lax.rem(lax.broadcasted_iota(jnp.int32, (queries, 1), 0) // heads, 8)
    get_nope.wait()
    get_absorb.wait()
    width = lat_vm.shape[2]

    def absorb(h, total):
        part_query = jnp.where(row_head == h, nope_vm[...], jnp.zeros((), jnp.bfloat16))
        return total + jnp.dot(part_query, absorb_vm[h], preferred_element_type=jnp.float32)

    absorbed = lax.fori_loop(0, heads, absorb, jnp.zeros((queries, width), jnp.float32))
    query[...] = absorbed.astype(jnp.bfloat16)
    get_qrope.wait()
    get_lat.wait()
    scale = 192.0**-0.5
    pair = 2 * TILE
    lane_row = lax.broadcasted_iota(jnp.int32, (1, TILE), 1)

    def score(i, peak):
        block = lat_vm[pl.ds(2 * i, 2)].reshape(pair, width)
        raw = lax.dot_general(
            query[...], block, (((1,), (1,)), ((), ())), preferred_element_type=jnp.float32
        )
        turned = []
        holders = []
        for b in range(2):
            turned.append(
                jnp.dot(qrope_vm[...], rope_vm[2 * i + b], preferred_element_type=jnp.float32)
            )
            g = lax.rem(me, per_row) * slots + 2 * i + b
            owner = owner_sm[me // per_row, g]
            left = length_sm[jnp.maximum(owner, 0)] - index_sm[me // per_row, g] * TILE
            holders.append(jnp.where(lane_row < left, owner, NEG))
        raw = (raw + jnp.concatenate(turned, axis=1)) * scale
        raw = jnp.where(jnp.concatenate(holders, axis=1) == row_request, raw, HIDDEN)
        scores[i] = raw
        return jnp.maximum(peak, raw)

    peak = lax.fori_loop(
        0, slots // 2, score, jnp.full((queries, pair), FLOOR, jnp.float32)
    )
    peak = jnp.max(peak, axis=1, keepdims=True)

    place(0)
    def weigh(i, carry):
        total, summed = carry
        weights = jnp.exp(scores[i] - peak)
        block = lat_vm[pl.ds(2 * i, 2)].reshape(pair, width)
        summed = summed + jnp.dot(
            weights.astype(jnp.bfloat16), block, preferred_element_type=jnp.float32
        )
        return total + weights, summed

    total, summed = lax.fori_loop(
        0,
        slots // 2,
        weigh,
        (jnp.zeros((queries, pair), jnp.float32), jnp.zeros((queries, width), jnp.float32)),
    )
    total = jnp.sum(total, axis=1, keepdims=True)
    query[...] = summed.astype(jnp.bfloat16)
    get_value.wait()

    def project(n, result):
        both = jnp.concatenate([value_vm[2 * n], value_vm[2 * n + 1]], axis=1)
        got = jnp.dot(query[...], both, preferred_element_type=jnp.float32)
        result = jnp.where(row_head == 2 * n, got[:, :TILE], result)
        return jnp.where(row_head == 2 * n + 1, got[:, TILE:], result)

    projected = lax.fori_loop(
        0, heads // 2, project, jnp.zeros((queries, TILE), jnp.float32)
    )
    wide = lax.broadcasted_iota(jnp.int32, (queries, TILE), 1)
    stats = jnp.where(
        wide < TILE // 2,
        jnp.broadcast_to(peak, (queries, TILE)),
        jnp.broadcast_to(total, (queries, TILE)),
    )
    x_send[:, 0] = projected.reshape(X, queries // X, TILE)
    x_send[:, 1] = stats.reshape(X, queries // X, TILE)
    x_got[x] = x_send[x]
    for k in range(1, X):
        peer = lax.rem(x + k, X)
        ship_part(x_send.at[peer], x_got.at[x], 0, z * X + peer)
    place(1)
    relay(0)

    wait_all(x_got, att_sem.at[0, 1])
    top, sums, totals = merge(x_got[...])
    z_send[:, 0] = sums.reshape(Z, 8, TILE)
    z_send[:, 1] = jnp.where(wide[: queries // X] < TILE // 2, top, totals).reshape(Z, 8, TILE)
    z_got[z] = z_send[z]
    for k in range(1, Z):
        peer = lax.rem(z + k, Z)
        ship_part(z_send.at[peer], z_got.at[z], 1, peer * X + x)
    place(2)
    relay(1)
    finish(0)

    wait_all(z_got, att_sem.at[1, 1])
    top, sums, totals = merge(z_got[...])
    z_all[z] = sums / totals
    for k in range(1, Z):
        ship_part(z_all.at[z], z_all.at[z], 2, lax.rem(z + k, Z) * X + x)
    place(3)
    relay(2)
    finish(1)
    wait_all(z_all, att_sem.at[2, 1])
    x_all[x] = z_all[...].reshape(queries // X, TILE)
    for k in range(1, X):
        ship_part(x_all.at[x], x_all.at[x], 3, z * X + lax.rem(x + k, X))
    relay(3)
    finish(2)
    wait_all(x_all, att_sem.at[3, 1])
    out_att[...] = x_all[...].reshape(queries, TILE)
    finish(3)

    for unit in range(parts + 1):
        arrived(unit, 0, y * 2 + other, None)
        arrived(unit, 3, o_down, None)
        arrived(unit, 4, o_up, None)
        arrived(unit, 7, o_far, 0)
        arrived(unit, 8, o_far, 1)
    for copy in started:
        copy.wait_send()
    for part in range(parts):
        wait_all(sends[part], a2a_send.at[part])
    wait_all(x_send, att_sem.at[0, 0])
    wait_all(z_send, att_sem.at[1, 0])
    wait_all(z_all, att_sem.at[2, 0])
    wait_all(x_all, att_sem.at[3, 0])


def hand_out(att, lat, rope, out_att, out_lat, out_rope, turned, sem):
    first = pltpu.make_async_copy(lat, out_lat, sem.at[0])
    first.start()
    second = pltpu.make_async_copy(att, out_att, sem.at[1])
    second.start()

    def turn(p, carry):
        for n in range(rope.shape[0] // 2):
            low = rope[2 * n, p].astype(jnp.float32)
            high = rope[2 * n + 1, p].astype(jnp.float32)
            for b in range(2):
                span = slice(8 * b, 8 * b + 8)
                both = jnp.concatenate([low[span], high[span]], axis=0)
                turned[2 * p + b, ROWS * n : ROWS * (n + 1), :] = both.astype(jnp.bfloat16)
        return carry

    lax.fori_loop(0, rope.shape[1], turn, 0, unroll=2)
    third = pltpu.make_async_copy(turned, out_rope, sem.at[2])
    third.start()
    first.wait()
    second.wait()
    third.wait()


def shards(
    latent_cache,
    rope_cache,
    query_nope,
    query_rope,
    key_absorb,
    value_up_weight,
    block_request,
    block_index,
    request_length,
    move_plan,
):
    slots, block, width = latent_cache.shape
    rope_width = rope_cache.shape[2]
    steps, requests, heads, nope_width = query_nope.shape
    queries = steps * requests * heads
    insts = lax.axis_size("inst")
    heads_axis = lax.axis_size("head")
    bf16, f32, i32 = jnp.bfloat16, jnp.float32, jnp.int32
    tiles = [
        2 * len(LANE_TILES[p]) + (1 if p == ROPE_CHUNK else 0) for p in range(len(LANE_TILES))
    ]
    units = len(LANE_TILES) + 1
    anywhere = pl.BlockSpec(memory_space=pl.ANY)
    attention, moved, rope = pl.pallas_call(
        kernel,
        out_shape=(
            pltpu.VMEM((queries, TILE), f32),
            pltpu.VMEM(latent_cache.shape, bf16),
            pltpu.VMEM((heads_axis, slots // 2, ROWS, TILE), bf16),
        ),
        in_specs=[pl.BlockSpec(memory_space=pltpu.HBM)] * 10,
        out_specs=(pl.BlockSpec(memory_space=pltpu.VMEM),) * 3,
        scratch_shapes=[
            pltpu.VMEM((slots, block, width), bf16),
            pltpu.VMEM((slots, rope_width, block), bf16),
            pltpu.VMEM((queries, nope_width), bf16),
            pltpu.VMEM((queries, rope_width), bf16),
            pltpu.VMEM(key_absorb.shape, bf16),
            pltpu.VMEM(value_up_weight.shape, bf16),
            pltpu.VMEM((8, TILE), i32),
            pltpu.SMEM((8, TILE), i32),
            pltpu.SMEM((8, TILE), i32),
            pltpu.SMEM((8,), i32),
            pltpu.VMEM((slots, TILE), i32),
            pltpu.SMEM((slots, TILE), i32),
            pltpu.VMEM((slots, ROWS, width), bf16),
            pltpu.VMEM((slots, 8, TILE), f32),
            pltpu.VMEM((slots, 8, TILE), f32),
            pltpu.VMEM((queries, width), bf16),
            pltpu.VMEM((slots // 2, queries, 2 * TILE), f32),
            pltpu.VMEM((X, 2, queries // X, TILE), f32),
            pltpu.VMEM((X, 2, queries // X, TILE), f32),
            pltpu.VMEM((Z, 2, 8, TILE), f32),
            pltpu.VMEM((Z, 2, 8, TILE), f32),
            pltpu.VMEM((Z, 8, TILE), f32),
            pltpu.VMEM((X, queries // X, TILE), f32),
        ]
        + [pltpu.VMEM((insts, n, ROWS, TILE), bf16) for n in tiles]
        + [pltpu.VMEM((insts, n, ROWS, TILE), bf16) for n in tiles]
        + [
            pltpu.SemaphoreType.DMA((12,)),
            pltpu.SemaphoreType.DMA((len(tiles),)),
            pltpu.SemaphoreType.DMA((len(tiles),)),
            pltpu.SemaphoreType.DMA((4, 2)),
            pltpu.SemaphoreType.DMA((units, 9)),
            pltpu.SemaphoreType.DMA((units, 9)),
        ],
        compiler_params=pltpu.CompilerParams(
            collective_id=0, has_side_effects=True, vmem_limit_bytes=40 * 2**20
        ),
        name="decode_and_move",
    )(
        *(
            pltpu.with_memory_space_constraint(a, pltpu.HBM)
            for a in (
                latent_cache,
                rope_cache.swapaxes(1, 2),
                query_nope.reshape(queries, nope_width),
                query_rope.reshape(queries, rope_width),
                key_absorb,
                value_up_weight,
                block_request.reshape(8, TILE),
                block_index.reshape(8, TILE),
                request_length,
                move_plan.reshape(8, TILE),
            )
        )
    )
    inside = [pltpu.with_memory_space_constraint(a, pltpu.VMEM) for a in (attention, moved, rope)]
    attention, moved, rope = pl.pallas_call(
        hand_out,
        out_shape=(
            jax.ShapeDtypeStruct((queries, TILE), f32),
            jax.ShapeDtypeStruct(latent_cache.shape, bf16),
            jax.ShapeDtypeStruct((slots, rope_width, block), bf16),
        ),
        in_specs=[pl.BlockSpec(memory_space=pltpu.VMEM)] * 3,
        out_specs=(anywhere,) * 3,
        scratch_shapes=[
            pltpu.VMEM((slots, rope_width, block), bf16),
            pltpu.SemaphoreType.DMA((3,)),
        ],
        compiler_params=pltpu.CompilerParams(vmem_limit_bytes=16 * 2**20),
        name="hand_out",
    )(*inside)
    attention = attention.reshape(steps, requests, heads, TILE)
    return attention, moved, rope.swapaxes(1, 2)


def solution(mesh):
    return jax.shard_map(
        shards,
        mesh=mesh,
        in_specs=(
            P("inst", None, None),
            P("inst", None, None),
            P(None, None, "head", None),
            P(None, None, "head", None),
            P("head", None, None),
            P("head", None, None),
            P(),
            P(),
            P(),
            P(),
        ),
        out_specs=(P(None, None, "head", None), P("inst", None, None), P("inst", None, None)),
        check_vma=False,
    )
```

```python
import functools

import jax
import jax.numpy as jnp
from jax import lax
from jax.experimental import pallas as pl
from jax.experimental.pallas import tpu as pltpu
from jax.sharding import PartitionSpec as P

MESH = pl.DeviceIdType.MESH
HIDDEN = -1e30
FLOOR = -1e29
TILE = 128
ROWS = 16
LANE_TILES = ((0,),(1,),(2,),(3,))
ROPE_CHUNK = 0
WINDOW = 9
PIECES = 8
Z, X = 8, 4
NEG = -1
ABSORB = 8
UNROLL = 4


def kernel(
    lat_hbm,
    rope_hbm,
    nope_hbm,
    qrope_hbm,
    absorb_hbm,
    value_hbm,
    owner_hbm,
    index_hbm,
    length_hbm,
    plan_hbm,
    out_att,
    out_lat,
    out_rope,
    lat_vm,
    rope_vm,
    nope_vm,
    qrope_vm,
    absorb_vm,
    value_vm,
    plan_vm,
    owner_sm,
    index_sm,
    length_sm,
    table_vm,
    table_sm,
    share,
    rope_share,
    rope_got,
    query,
    scores,
    x_send,
    x_got,
    z_send,
    z_got,
    z_all,
    x_all,
    *rest,

):
    parts = len(LANE_TILES)
    sends, gots = rest[:parts], rest[parts : 2 * parts]
    in_sem, a2a_send, a2a_recv, att_sem, ag_send, ag_recv = rest[2 * parts :]
    insts = lax.axis_size("inst")
    me = lax.axis_index("inst")
    head = lax.axis_index("head")
    core = lax.rem(head, 2)
    y = head // 2
    up = lax.rem(y + 1, 4)
    down = lax.rem(y + 3, 4)
    far = lax.rem(y + 2, 4)
    other = 1 - core
    slots = lat_vm.shape[0]
    z, x = me // X, lax.rem(me, X)

    def fetch(k, source, target):
        copy = pltpu.make_async_copy(source, target, in_sem.at[k])
        copy.start()
        return copy

    rows = pl.ds(pl.multiple_of(head * ROWS, ROWS), ROWS)
    get_plan = fetch(0, plan_hbm, plan_vm)
    get_share = fetch(1, lat_hbm.at[:, rows, :], share)
    get_rope = fetch(2, rope_hbm, rope_vm)
    get_owner = fetch(3, owner_hbm, owner_sm)
    get_index = fetch(4, index_hbm, index_sm)
    get_length = fetch(5, length_hbm, length_sm)
    get_nope = fetch(6, nope_hbm, nope_vm)
    get_absorb = fetch(7, absorb_hbm, absorb_vm)
    get_qrope = fetch(8, qrope_hbm, qrope_vm)
    get_lat = fetch(9, lat_hbm, lat_vm)
    get_value = fetch(10, value_hbm, value_vm)

    barrier = pltpu.get_barrier_semaphore()

    def greet(k, carry):
        pl.semaphore_signal(
            barrier,
            inc=1,
            device_id={"inst": lax.rem(me + k, insts)},
            device_id_type=MESH,
        )
        return carry

    lax.fori_loop(1, insts, greet, 0)
    mates = (y * 2 + other, up * 2 + core, down * 2 + core, far * 2 + core)
    for mate in mates:
        pl.semaphore_signal(barrier, inc=1, device_id={"head": mate}, device_id_type=MESH)

    get_plan.wait()
    plan = plan_vm[...]
    lane = lax.broadcasted_iota(jnp.int32, (8, TILE), 1)
    row = lax.broadcasted_iota(jnp.int32, (8, TILE), 0)
    per_row = TILE // slots
    group = lane // slots
    within = lane - group * slots
    seen = jnp.where((plan >> 5) == me, 1, 0)
    for d in (1, 2, 4, 8, 16):
        seen = jnp.maximum(seen, jnp.where(within >= d, pltpu.roll(seen, d, 1), 0))
    rank = jnp.where(within >= 1, pltpu.roll(seen, 1, 1), 0)
    code = (row * per_row + group) * 2 + rank
    column = lax.broadcasted_iota(jnp.int32, (slots, TILE), 0)
    lanes = lax.broadcasted_iota(jnp.int32, (slots, TILE), 1)
    hit = jnp.full((slots, TILE), NEG, jnp.int32)
    for r in range(8):
        wanted = jnp.broadcast_to(plan[r : r + 1, :], (slots, TILE)) == me * slots + column
        hit = jnp.maximum(
            hit, jnp.where(wanted, jnp.broadcast_to(code[r : r + 1, :], (slots, TILE)), NEG)
        )
    land = jnp.max(hit, axis=1, keepdims=True)
    mine = plan_vm[pl.ds(me // per_row, 1), :]
    own_lane = lax.rem(me, per_row) * slots + column
    own = jnp.max(
        jnp.where(lanes == own_lane, jnp.broadcast_to(mine, (slots, TILE)), NEG),
        axis=1,
        keepdims=True,
    )
    mine = jnp.where(group[:1] == lax.rem(me, per_row), mine >> 5, NEG)
    goes = jnp.broadcast_to(mine, (slots, TILE)) == column
    place = lanes - lanes // slots * slots
    first = jnp.min(jnp.where(goes, place, slots), axis=1, keepdims=True)
    last = jnp.max(jnp.where(goes, place, 0), axis=1, keepdims=True)
    first = jnp.where(first >= slots, 0, first)
    table_vm[...] = jnp.where(
        lanes == 0,
        jnp.broadcast_to(first, (slots, TILE)),
        jnp.where(
            lanes == 1,
            jnp.broadcast_to(last, (slots, TILE)),
            jnp.where(
                lanes == 2,
                jnp.broadcast_to(land, (slots, TILE)),
                jnp.broadcast_to(own, (slots, TILE)),
            ),
        ),
    )
    get_table = fetch(11, table_vm, table_sm)

    get_rope.wait()
    half = pl.ds(pl.multiple_of(y * ROWS, ROWS), ROWS)

    def cut_rope(t, carry):
        piece = rope_vm[t, half, :].astype(jnp.float32)
        rope_share[t] = jnp.where(core == 0, piece[:8], piece[8:])
        return carry

    lax.fori_loop(0, slots, cut_rope, 0, unroll=4)
    get_share.wait()
    get_table.wait()
    get_owner.wait()
    get_index.wait()
    get_length.wait()

    def dispatch(part):
        if part >= parts:
            return
        tiles = LANE_TILES[part]
        count = len(tiles)
        buffer = sends[part]

        def pack(j, carry):
            picks = (table_sm[j, 0], table_sm[j, 1])
            for seat in range(2):
                for n, tile in enumerate(tiles):
                    buffer[j, seat * count + n] = share[
                        picks[seat], :, tile * TILE : (tile + 1) * TILE
                    ]
            if part == ROPE_CHUNK:
                buffer[j, 2 * count] = jnp.concatenate(
                    [rope_share[picks[0]], rope_share[picks[1]]], axis=0
                ).astype(jnp.bfloat16)
            return carry

        lax.fori_loop(0, insts, pack, 0, unroll=4)
        if part == 0:
            pl.semaphore_wait(barrier, insts - 1 + len(mates))

        def ship(k, carry):
            peer = lax.rem(me + k, insts)
            pltpu.make_async_remote_copy(
                src_ref=buffer.at[peer],
                dst_ref=gots[part].at[me],
                send_sem=a2a_send.at[part],
                recv_sem=a2a_recv.at[part],
                device_id={"inst": peer},
                device_id_type=MESH,
            ).start()
            return carry

        lax.fori_loop(1, insts, ship, 0)

    for part in range(min(WINDOW, parts)):
        dispatch(part)

    def wait_all(buffer, sem):
        whole = buffer.at[pl.ds(0, buffer.shape[0] - 1)]
        pltpu.make_async_copy(whole, whole, sem).wait()

    def ship_part(source, target, k, peer):
        pltpu.make_async_remote_copy(
            src_ref=source,
            dst_ref=target,
            send_sem=att_sem.at[k, 0],
            recv_sem=att_sem.at[k, 1],
            device_id={"inst": peer},
            device_id_type=MESH,
        ).start()

    def merge(got):
        partial, stat = got[:, 0], got[:, 1]
        peaks, totals = stat[:, :, :1], stat[:, :, TILE // 2 : TILE // 2 + 1]
        top = jnp.max(peaks, axis=0, keepdims=True)
        weight = jnp.exp(peaks - top)
        return top[0], jnp.sum(partial * weight, axis=0), jnp.sum(totals * weight, axis=0)

    def region(unit, h, which):
        n = slots if unit < parts else slots // 2
        span = {
            None: pl.ds(0, n),
            0: pl.ds(0, n // 2),
            1: pl.ds(n // 2, n // 2),
        }[which]
        if unit < parts:
            tiles = LANE_TILES[unit]
            return out_lat.at[
                span,
                pl.ds(pl.multiple_of(h * ROWS, ROWS), ROWS),
                pl.ds(tiles[0] * TILE, len(tiles) * TILE),
            ]
        return out_rope.at[h, span]

    started = []

    def send(unit, k, source, h, which, mate):
        copy = pltpu.make_async_remote_copy(
            src_ref=source,
            dst_ref=region(unit, h, which),
            send_sem=ag_send.at[unit, k],
            recv_sem=ag_recv.at[unit, k],
            device_id={"head": mate},
            device_id_type=MESH,
        )
        copy.start()
        started.append(copy)

    def arrived(unit, k, h, which):
        here = region(unit, h, which)
        pltpu.make_async_copy(here, here, ag_recv.at[unit, k]).wait()

    side, above, below, _ = mates
    h_up, h_down, h_far = up * 2 + core, down * 2 + core, far * 2 + core
    o_up, o_down, o_far = up * 2 + other, down * 2 + other, far * 2 + other
    extra = {p: [p] * (len(LANE_TILES[p]) > 0) + [parts] * (p == ROPE_CHUNK) for p in range(parts)}
    units = [unit for p in range(parts) for unit in extra[p]]

    def place(part):
        tiles = LANE_TILES[part]
        count = len(tiles)
        buffer = gots[part]
        wait_all(buffer, a2a_recv.at[part])
        dispatch(part + WINDOW)

        def put(t, carry):
            where = table_sm[t, 2]
            g = lax.rem(me, per_row) * slots + t
            keep = (owner_sm[me // per_row, g] >= 0) & (table_sm[t, 3] < 0)
            spot = jnp.maximum(where, 0)
            source, seat = spot // 2, lax.rem(spot, 2)
            for n, tile in enumerate(tiles):
                span = slice(tile * TILE, (tile + 1) * TILE)
                moved = buffer[source, seat * count + n]
                kept = share[t, :, span]
                zero = jnp.zeros_like(moved)
                out_lat[t, rows, span] = jnp.where(
                    keep, kept, jnp.where(where >= 0, moved, zero)
                )
            if part == ROPE_CHUNK:
                pieces = buffer[source, 2 * count].astype(jnp.float32)
                moved = jnp.where(seat == 0, pieces[:8], pieces[8:])
                zero = jnp.zeros_like(moved)
                rope_got[t] = jnp.where(
                    keep, rope_share[t], jnp.where(where >= 0, moved, zero)
                )
            return carry

        lax.fori_loop(0, slots, put, 0, unroll=4)
        if part == ROPE_CHUNK:
            out_rope[head] = rope_got[...].reshape(slots // 2, ROWS, TILE).astype(jnp.bfloat16)
        for unit in extra[part]:
            source = region(unit, head, None)
            send(unit, 1, source, head, None, above)
            send(unit, 2, source, head, None, below)
            if part == parts - 1:
                send(unit, 5, source, head, None, far * 2 + core)
            send(unit, 0, source, head, None, side)

    def relay(part):
        if part == parts - 1:
            for unit in extra[part]:
                arrived(unit, 1, h_down, None)
                send(unit, 3, region(unit, h_down, None), h_down, None, side)
                arrived(unit, 2, h_up, None)
                send(unit, 4, region(unit, h_up, None), h_up, None, side)
            return
        for unit in extra[part]:
            arrived(unit, 1, h_down, None)
            send(unit, 5, region(unit, h_down, 0), h_down, 0, above)
            send(unit, 3, region(unit, h_down, None), h_down, None, side)
            arrived(unit, 2, h_up, None)
            send(unit, 6, region(unit, h_up, 1), h_up, 1, below)
            send(unit, 4, region(unit, h_up, None), h_up, None, side)

    def finish(part):
        if part == parts - 1:
            for unit in extra[part]:
                arrived(unit, 5, h_far, None)
                send(unit, 7, region(unit, h_far, None), h_far, None, side)
            return
        for unit in extra[part]:
            arrived(unit, 5, h_far, 0)
            send(unit, 7, region(unit, h_far, 0), h_far, 0, side)
            arrived(unit, 6, h_far, 1)
            send(unit, 8, region(unit, h_far, 1), h_far, 1, side)

    heads = 16
    queries = nope_vm.shape[0]
    row_head = lax.rem(lax.broadcasted_iota(jnp.int32, (queries, 1), 0), heads)
    row_request = lax.rem(lax.broadcasted_iota(jnp.int32, (queries, 1), 0) // heads, 8)
    get_nope.wait()
    get_absorb.wait()
    width = lat_vm.shape[2]

    def absorb(n, total):
        part_query = [
            jnp.where(row_head == ABSORB * n + h, nope_vm[...], jnp.zeros((), jnp.bfloat16))
            for h in range(ABSORB)
        ]
        weights = absorb_vm[pl.ds(ABSORB * n, ABSORB)].reshape(ABSORB * TILE, width)
        return total + jnp.dot(
            jnp.concatenate(part_query, axis=1), weights, preferred_element_type=jnp.float32
        )

    absorbed = lax.fori_loop(
        0, heads // ABSORB, absorb, jnp.zeros((queries, width), jnp.float32)
    )
    query[...] = absorbed.astype(jnp.bfloat16)
    get_qrope.wait()
    get_lat.wait()
    scale = 192.0**-0.5
    pair = 2 * TILE
    lane_row = lax.broadcasted_iota(jnp.int32, (1, TILE), 1)

    def score(i, peak):
        block = lat_vm[pl.ds(2 * i, 2)].reshape(pair, width)
        raw = lax.dot_general(
            query[...], block, (((1,), (1,)), ((), ())), preferred_element_type=jnp.float32
        )
        turned = []
        holders = []
        for b in range(2):
            turned.append(
                jnp.dot(qrope_vm[...], rope_vm[2 * i + b], preferred_element_type=jnp.float32)
            )
            g = lax.rem(me, per_row) * slots + 2 * i + b
            owner = owner_sm[me // per_row, g]
            left = length_sm[jnp.maximum(owner, 0)] - index_sm[me // per_row, g] * TILE
            holders.append(jnp.where(lane_row < left, owner, NEG))
        raw = (raw + jnp.concatenate(turned, axis=1)) * scale
        raw = jnp.where(jnp.concatenate(holders, axis=1) == row_request, raw, HIDDEN)
        scores[i] = raw
        return jnp.maximum(peak, raw)

    peak = lax.fori_loop(
        0, slots // 2, score, jnp.full((queries, pair), FLOOR, jnp.float32), unroll=UNROLL
    )
    peak = jnp.max(peak, axis=1, keepdims=True)

    def weigh(i, carry):
        total, summed = carry
        weights = jnp.exp(scores[i] - peak)
        block = lat_vm[pl.ds(2 * i, 2)].reshape(pair, width)
        summed = summed + jnp.dot(
            weights.astype(jnp.bfloat16), block, preferred_element_type=jnp.float32
        )
        return total + weights, summed

    total, summed = lax.fori_loop(
        0,
        slots // 2,
        weigh,
        (jnp.zeros((queries, pair), jnp.float32), jnp.zeros((queries, width), jnp.float32)),
        unroll=UNROLL,
    )
    total = jnp.sum(total, axis=1, keepdims=True)
    query[...] = summed.astype(jnp.bfloat16)
    get_value.wait()

    def project(n, result):
        both = jnp.concatenate([value_vm[2 * n], value_vm[2 * n + 1]], axis=1)
        got = jnp.dot(query[...], both, preferred_element_type=jnp.float32)
        result = jnp.where(row_head == 2 * n, got[:, :TILE], result)
        return jnp.where(row_head == 2 * n + 1, got[:, TILE:], result)

    projected = lax.fori_loop(
        0, heads // 2, project, jnp.zeros((queries, TILE), jnp.float32), unroll=UNROLL
    )
    wide = lax.broadcasted_iota(jnp.int32, (queries, TILE), 1)
    stats = jnp.where(
        wide < TILE // 2,
        jnp.broadcast_to(peak, (queries, TILE)),
        jnp.broadcast_to(total, (queries, TILE)),
    )
    x_send[:, 0] = projected.reshape(X, queries // X, TILE)
    x_send[:, 1] = stats.reshape(X, queries // X, TILE)
    x_got[x] = x_send[x]
    for k in range(1, X):
        peer = lax.rem(x + k, X)
        ship_part(x_send.at[peer], x_got.at[x], 0, z * X + peer)
    place(0)
    place(1)
    relay(0)

    wait_all(x_got, att_sem.at[0, 1])
    top, sums, totals = merge(x_got[...])
    z_send[:, 0] = sums.reshape(Z, 8, TILE)
    z_send[:, 1] = jnp.where(wide[: queries // X] < TILE // 2, top, totals).reshape(Z, 8, TILE)
    z_got[z] = z_send[z]
    for k in range(1, Z):
        peer = lax.rem(z + k, Z)
        ship_part(z_send.at[peer], z_got.at[z], 1, peer * X + x)

    def second():
        wait_all(z_got, att_sem.at[1, 1])
        top, sums, totals = merge(z_got[...])
        z_all[z] = sums / totals
        for k in range(1, Z):
            ship_part(z_all.at[z], z_all.at[z], 2, lax.rem(z + k, Z) * X + x)

    def third():
        wait_all(z_all, att_sem.at[2, 1])
        x_all[x] = z_all[...].reshape(queries // X, TILE)
        for k in range(1, X):
            ship_part(x_all.at[x], x_all.at[x], 3, z * X + lax.rem(x + k, X))

    for part in range(2, parts):
        relay(part - 1)
        place(part)
        finish(part - 2)
        if part == 2:
            second()
        if part == 3:
            third()
    relay(parts - 1)
    finish(parts - 2)
    if parts <= 3:
        third()
    finish(parts - 1)
    wait_all(x_all, att_sem.at[3, 1])
    out_att[...] = x_all[...].reshape(queries, TILE)

    for unit in units:
        arrived(unit, 0, y * 2 + other, None)
        arrived(unit, 3, o_down, None)
        arrived(unit, 4, o_up, None)
        if unit in extra[parts - 1]:
            arrived(unit, 7, o_far, None)
        else:
            arrived(unit, 7, o_far, 0)
            arrived(unit, 8, o_far, 1)
    for copy in started:
        copy.wait_send()
    for part in range(parts):
        wait_all(sends[part], a2a_send.at[part])
    wait_all(x_send, att_sem.at[0, 0])
    wait_all(z_send, att_sem.at[1, 0])
    wait_all(z_all, att_sem.at[2, 0])
    wait_all(x_all, att_sem.at[3, 0])


def hand_out(att, lat, rope, out_att, out_lat, out_rope, turned, sem):
    step = lat.shape[0] // PIECES
    copies = []
    for n in range(PIECES):
        span = pl.ds(n * step, step)
        copies.append(pltpu.make_async_copy(lat.at[span], out_lat.at[span], sem.at[3 + n]))
        copies[-1].start()
    second = pltpu.make_async_copy(att, out_att, sem.at[1])
    second.start()

    def turn(p, carry):
        for n in range(rope.shape[0] // 2):
            low = rope[2 * n, p].astype(jnp.float32)
            high = rope[2 * n + 1, p].astype(jnp.float32)
            for b in range(2):
                span = slice(8 * b, 8 * b + 8)
                both = jnp.concatenate([low[span], high[span]], axis=0)
                turned[2 * p + b, ROWS * n : ROWS * (n + 1), :] = both.astype(jnp.bfloat16)
        return carry

    lax.fori_loop(0, rope.shape[1], turn, 0, unroll=2)
    third = pltpu.make_async_copy(turned, out_rope, sem.at[2])
    third.start()
    for copy in copies:
        copy.wait()
    second.wait()
    third.wait()


def shards(
    latent_cache,
    rope_cache,
    query_nope,
    query_rope,
    key_absorb,
    value_up_weight,
    block_request,
    block_index,
    request_length,
    move_plan,
):
    slots, block, width = latent_cache.shape
    rope_width = rope_cache.shape[2]
    steps, requests, heads, nope_width = query_nope.shape
    queries = steps * requests * heads
    insts = lax.axis_size("inst")
    heads_axis = lax.axis_size("head")
    bf16, f32, i32 = jnp.bfloat16, jnp.float32, jnp.int32
    tiles = [
        2 * len(LANE_TILES[p]) + (1 if p == ROPE_CHUNK else 0) for p in range(len(LANE_TILES))
    ]
    units = len(LANE_TILES) + 1
    anywhere = pl.BlockSpec(memory_space=pl.ANY)
    attention, moved, rope = pl.pallas_call(
        kernel,
        out_shape=(
            pltpu.VMEM((queries, TILE), f32),
            pltpu.VMEM(latent_cache.shape, bf16),
            pltpu.VMEM((heads_axis, slots // 2, ROWS, TILE), bf16),
        ),
        in_specs=[pl.BlockSpec(memory_space=pltpu.HBM)] * 10,
        out_specs=(pl.BlockSpec(memory_space=pltpu.VMEM),) * 3,
        scratch_shapes=[
            pltpu.VMEM((slots, block, width), bf16),
            pltpu.VMEM((slots, rope_width, block), bf16),
            pltpu.VMEM((queries, nope_width), bf16),
            pltpu.VMEM((queries, rope_width), bf16),
            pltpu.VMEM(key_absorb.shape, bf16),
            pltpu.VMEM(value_up_weight.shape, bf16),
            pltpu.VMEM((8, TILE), i32),
            pltpu.SMEM((8, TILE), i32),
            pltpu.SMEM((8, TILE), i32),
            pltpu.SMEM((8,), i32),
            pltpu.VMEM((slots, TILE), i32),
            pltpu.SMEM((slots, TILE), i32),
            pltpu.VMEM((slots, ROWS, width), bf16),
            pltpu.VMEM((slots, 8, TILE), f32),
            pltpu.VMEM((slots, 8, TILE), f32),
            pltpu.VMEM((queries, width), bf16),
            pltpu.VMEM((slots // 2, queries, 2 * TILE), f32),
            pltpu.VMEM((X, 2, queries // X, TILE), f32),
            pltpu.VMEM((X, 2, queries // X, TILE), f32),
            pltpu.VMEM((Z, 2, 8, TILE), f32),
            pltpu.VMEM((Z, 2, 8, TILE), f32),
            pltpu.VMEM((Z, 8, TILE), f32),
            pltpu.VMEM((X, queries // X, TILE), f32),
        ]
        + [pltpu.VMEM((insts, n, ROWS, TILE), bf16) for n in tiles]
        + [pltpu.VMEM((insts, n, ROWS, TILE), bf16) for n in tiles]
        + [
            pltpu.SemaphoreType.DMA((12,)),
            pltpu.SemaphoreType.DMA((len(tiles),)),
            pltpu.SemaphoreType.DMA((len(tiles),)),
            pltpu.SemaphoreType.DMA((4, 2)),
            pltpu.SemaphoreType.DMA((units, 9)),
            pltpu.SemaphoreType.DMA((units, 9)),
        ],
        compiler_params=pltpu.CompilerParams(
            collective_id=0, has_side_effects=True, vmem_limit_bytes=40 * 2**20
        ),
        name="decode_and_move",
    )(
        *(
            pltpu.with_memory_space_constraint(a, pltpu.HBM)
            for a in (
                latent_cache,
                rope_cache.swapaxes(1, 2),
                query_nope.reshape(queries, nope_width),
                query_rope.reshape(queries, rope_width),
                key_absorb,
                value_up_weight,
                block_request.reshape(8, TILE),
                block_index.reshape(8, TILE),
                request_length,
                move_plan.reshape(8, TILE),
            )
        )
    )
    inside = [pltpu.with_memory_space_constraint(a, pltpu.VMEM) for a in (attention, moved, rope)]
    attention, moved, rope = pl.pallas_call(
        hand_out,
        out_shape=(
            jax.ShapeDtypeStruct((queries, TILE), f32),
            jax.ShapeDtypeStruct(latent_cache.shape, bf16),
            jax.ShapeDtypeStruct((slots, rope_width, block), bf16),
        ),
        in_specs=[pl.BlockSpec(memory_space=pltpu.VMEM)] * 3,
        out_specs=(anywhere,) * 3,
        scratch_shapes=[
            pltpu.VMEM((slots, rope_width, block), bf16),
            pltpu.SemaphoreType.DMA((3 + PIECES,)),
        ],
        compiler_params=pltpu.CompilerParams(vmem_limit_bytes=16 * 2**20),
        name="hand_out",
    )(*inside)
    attention = attention.reshape(steps, requests, heads, TILE)
    return attention, moved, rope.swapaxes(1, 2)


def solution(mesh):
    return jax.shard_map(
        shards,
        mesh=mesh,
        in_specs=(
            P("inst", None, None),
            P("inst", None, None),
            P(None, None, "head", None),
            P(None, None, "head", None),
            P("head", None, None),
            P("head", None, None),
            P(),
            P(),
            P(),
            P(),
        ),
        out_specs=(P(None, None, "head", None), P("inst", None, None), P("inst", None, None)),
        check_vma=False,
    )
```

```python
import functools

import jax
import jax.numpy as jnp
from jax import lax
from jax.experimental import pallas as pl
from jax.experimental.pallas import tpu as pltpu
from jax.sharding import PartitionSpec as P

MESH = pl.DeviceIdType.MESH
HIDDEN = -1e30
FLOOR = -1e29
TILE = 128
ROWS = 16
LANE_TILES = ((0,),(1,),(2,),(3,))
ROPE_CHUNK = 0
WINDOW = 2
PIECES = 8
Z, X = 8, 4
ROW_ORDER = (0, 1, 2, 3, 7, 4, 5, 6)
NEG = -1
ABSORB = 8
UNROLL = 4


def kernel(
    lat_hbm,
    rope_hbm,
    nope_hbm,
    qrope_hbm,
    absorb_hbm,
    value_hbm,
    owner_hbm,
    index_hbm,
    length_hbm,
    plan_hbm,
    out_att,
    out_lat,
    out_rope,
    lat_vm,
    rope_vm,
    nope_vm,
    qrope_vm,
    absorb_vm,
    value_vm,
    plan_vm,
    owner_sm,
    index_sm,
    length_sm,
    table_vm,
    table_sm,
    share,
    rope_share,
    rope_got,
    query,
    scores,
    x_send,
    x_got,
    z_send,
    z_got,
    z_all,
    x_all,
    *rest,

):
    parts = len(LANE_TILES)
    sends, gots = rest[:parts], rest[parts : 2 * parts]
    in_sem, a2a_send, a2a_recv, att_sem, ag_send, ag_recv = rest[2 * parts :]
    insts = lax.axis_size("inst")
    me = lax.axis_index("inst")
    head = lax.axis_index("head")
    core = lax.rem(head, 2)
    y = head // 2
    up = lax.rem(y + 1, 4)
    down = lax.rem(y + 3, 4)
    far = lax.rem(y + 2, 4)
    other = 1 - core
    slots = lat_vm.shape[0]
    z, x = me // X, lax.rem(me, X)

    def fetch(k, source, target):
        copy = pltpu.make_async_copy(source, target, in_sem.at[k])
        copy.start()
        return copy

    rows = pl.ds(pl.multiple_of(head * ROWS, ROWS), ROWS)
    get_plan = fetch(0, plan_hbm, plan_vm)
    get_share = fetch(1, lat_hbm.at[:, rows, :], share)
    get_rope = fetch(2, rope_hbm, rope_vm)
    get_owner = fetch(3, owner_hbm, owner_sm)
    get_index = fetch(4, index_hbm, index_sm)
    get_length = fetch(5, length_hbm, length_sm)
    get_nope = fetch(6, nope_hbm, nope_vm)
    get_absorb = fetch(7, absorb_hbm, absorb_vm)
    get_qrope = fetch(8, qrope_hbm, qrope_vm)
    get_lat = fetch(9, lat_hbm, lat_vm)
    get_value = fetch(10, value_hbm, value_vm)

    barrier = pltpu.get_barrier_semaphore()

    def greet(k, carry):
        pl.semaphore_signal(
            barrier,
            inc=1,
            device_id={"inst": lax.rem(me + k, insts)},
            device_id_type=MESH,
        )
        return carry

    lax.fori_loop(1, insts, greet, 0)
    mates = (y * 2 + other, up * 2 + core, down * 2 + core, far * 2 + core)
    for mate in mates:
        pl.semaphore_signal(barrier, inc=1, device_id={"head": mate}, device_id_type=MESH)

    get_plan.wait()
    plan = plan_vm[...]
    lane = lax.broadcasted_iota(jnp.int32, (8, TILE), 1)
    row = lax.broadcasted_iota(jnp.int32, (8, TILE), 0)
    per_row = TILE // slots
    group = lane // slots
    within = lane - group * slots
    seen = jnp.where((plan >> 5) == me, 1, 0)
    for d in (1, 2, 4, 8, 16):
        seen = jnp.maximum(seen, jnp.where(within >= d, pltpu.roll(seen, d, 1), 0))
    rank = jnp.where(within >= 1, pltpu.roll(seen, 1, 1), 0)
    code = (row * per_row + group) * 2 + rank
    column = lax.broadcasted_iota(jnp.int32, (slots, TILE), 0)
    lanes = lax.broadcasted_iota(jnp.int32, (slots, TILE), 1)
    hit = jnp.full((slots, TILE), NEG, jnp.int32)
    for r in range(8):
        wanted = jnp.broadcast_to(plan[r : r + 1, :], (slots, TILE)) == me * slots + column
        hit = jnp.maximum(
            hit, jnp.where(wanted, jnp.broadcast_to(code[r : r + 1, :], (slots, TILE)), NEG)
        )
    land = jnp.max(hit, axis=1, keepdims=True)
    mine = plan_vm[pl.ds(me // per_row, 1), :]
    own_lane = lax.rem(me, per_row) * slots + column
    own = jnp.max(
        jnp.where(lanes == own_lane, jnp.broadcast_to(mine, (slots, TILE)), NEG),
        axis=1,
        keepdims=True,
    )
    mine = jnp.where(group[:1] == lax.rem(me, per_row), mine >> 5, NEG)
    goes = jnp.broadcast_to(mine, (slots, TILE)) == column
    place = lanes - lanes // slots * slots
    first = jnp.min(jnp.where(goes, place, slots), axis=1, keepdims=True)
    last = jnp.max(jnp.where(goes, place, 0), axis=1, keepdims=True)
    first = jnp.where(first >= slots, 0, first)
    table_vm[...] = jnp.where(
        lanes == 0,
        jnp.broadcast_to(first, (slots, TILE)),
        jnp.where(
            lanes == 1,
            jnp.broadcast_to(last, (slots, TILE)),
            jnp.where(
                lanes == 2,
                jnp.broadcast_to(land, (slots, TILE)),
                jnp.broadcast_to(own, (slots, TILE)),
            ),
        ),
    )
    get_table = fetch(11, table_vm, table_sm)

    get_rope.wait()
    half = pl.ds(pl.multiple_of(y * ROWS, ROWS), ROWS)

    def cut_rope(t, carry):
        piece = rope_vm[t, half, :].astype(jnp.float32)
        rope_share[t] = jnp.where(core == 0, piece[:8], piece[8:])
        return carry

    lax.fori_loop(0, slots, cut_rope, 0, unroll=4)
    get_share.wait()
    get_table.wait()
    get_owner.wait()
    get_index.wait()
    get_length.wait()

    def dispatch(part):
        if part >= parts:
            return
        tiles = LANE_TILES[part]
        count = len(tiles)
        buffer = sends[part]

        def pack(j, carry):
            picks = (table_sm[j, 0], table_sm[j, 1])
            for seat in range(2):
                for n, tile in enumerate(tiles):
                    buffer[j, seat * count + n] = share[
                        picks[seat], :, tile * TILE : (tile + 1) * TILE
                    ]
            if part == ROPE_CHUNK:
                buffer[j, 2 * count] = jnp.concatenate(
                    [rope_share[picks[0]], rope_share[picks[1]]], axis=0
                ).astype(jnp.bfloat16)
            return carry

        lax.fori_loop(0, insts, pack, 0, unroll=4)
        if part == 0:
            pl.semaphore_wait(barrier, insts - 1 + len(mates))

        def ship(k, carry):
            peer = carry * X + lax.rem(x + k, X)

            @pl.when(peer != me)
            def _():
                pltpu.make_async_remote_copy(
                    src_ref=buffer.at[peer],
                    dst_ref=gots[part].at[me],
                    send_sem=a2a_send.at[part],
                    recv_sem=a2a_recv.at[part],
                    device_id={"inst": peer},
                    device_id_type=MESH,
                ).start()

            return carry

        for row in ROW_ORDER:
            lax.fori_loop(0, X, ship, row)

    for part in range(min(WINDOW, parts)):
        dispatch(part)

    def wait_all(buffer, sem):
        whole = buffer.at[pl.ds(0, buffer.shape[0] - 1)]
        pltpu.make_async_copy(whole, whole, sem).wait()

    def ship_part(source, target, k, peer):
        pltpu.make_async_remote_copy(
            src_ref=source,
            dst_ref=target,
            send_sem=att_sem.at[k, 0],
            recv_sem=att_sem.at[k, 1],
            device_id={"inst": peer},
            device_id_type=MESH,
        ).start()

    def merge(got):
        partial, stat = got[:, 0], got[:, 1]
        peaks, totals = stat[:, :, :1], stat[:, :, TILE // 2 : TILE // 2 + 1]
        top = jnp.max(peaks, axis=0, keepdims=True)
        weight = jnp.exp(peaks - top)
        return top[0], jnp.sum(partial * weight, axis=0), jnp.sum(totals * weight, axis=0)

    def region(unit, h, which):
        n = slots if unit < parts else slots // 2
        span = {
            None: pl.ds(0, n),
            0: pl.ds(0, n // 2),
            1: pl.ds(n // 2, n // 2),
        }[which]
        if unit < parts:
            tiles = LANE_TILES[unit]
            return out_lat.at[
                span,
                pl.ds(pl.multiple_of(h * ROWS, ROWS), ROWS),
                pl.ds(tiles[0] * TILE, len(tiles) * TILE),
            ]
        return out_rope.at[h, span]

    started = []

    def send(unit, k, source, h, which, mate):
        copy = pltpu.make_async_remote_copy(
            src_ref=source,
            dst_ref=region(unit, h, which),
            send_sem=ag_send.at[unit, k],
            recv_sem=ag_recv.at[unit, k],
            device_id={"head": mate},
            device_id_type=MESH,
        )
        copy.start()
        started.append(copy)

    def arrived(unit, k, h, which):
        here = region(unit, h, which)
        pltpu.make_async_copy(here, here, ag_recv.at[unit, k]).wait()

    side, above, below, _ = mates
    h_up, h_down, h_far = up * 2 + core, down * 2 + core, far * 2 + core
    o_up, o_down, o_far = up * 2 + other, down * 2 + other, far * 2 + other
    extra = {p: [p] * (len(LANE_TILES[p]) > 0) + [parts] * (p == ROPE_CHUNK) for p in range(parts)}
    units = [unit for p in range(parts) for unit in extra[p]]

    def place(part):
        tiles = LANE_TILES[part]
        count = len(tiles)
        buffer = gots[part]
        wait_all(buffer, a2a_recv.at[part])
        dispatch(part + WINDOW)

        def put(t, carry):
            where = table_sm[t, 2]
            g = lax.rem(me, per_row) * slots + t
            keep = (owner_sm[me // per_row, g] >= 0) & (table_sm[t, 3] < 0)
            spot = jnp.maximum(where, 0)
            source, seat = spot // 2, lax.rem(spot, 2)
            for n, tile in enumerate(tiles):
                span = slice(tile * TILE, (tile + 1) * TILE)
                moved = buffer[source, seat * count + n]
                kept = share[t, :, span]
                zero = jnp.zeros_like(moved)
                out_lat[t, rows, span] = jnp.where(
                    keep, kept, jnp.where(where >= 0, moved, zero)
                )
            if part == ROPE_CHUNK:
                pieces = buffer[source, 2 * count].astype(jnp.float32)
                moved = jnp.where(seat == 0, pieces[:8], pieces[8:])
                zero = jnp.zeros_like(moved)
                rope_got[t] = jnp.where(
                    keep, rope_share[t], jnp.where(where >= 0, moved, zero)
                )
            return carry

        lax.fori_loop(0, slots, put, 0, unroll=4)
        if part == ROPE_CHUNK:
            out_rope[head] = rope_got[...].reshape(slots // 2, ROWS, TILE).astype(jnp.bfloat16)
        for unit in extra[part]:
            source = region(unit, head, None)
            send(unit, 1, source, head, None, above)
            send(unit, 2, source, head, None, below)
            if part == parts - 1:
                send(unit, 5, source, head, None, far * 2 + core)
            send(unit, 0, source, head, None, side)

    def relay(part):
        if part == parts - 1:
            for unit in extra[part]:
                arrived(unit, 1, h_down, None)
                send(unit, 3, region(unit, h_down, None), h_down, None, side)
                arrived(unit, 2, h_up, None)
                send(unit, 4, region(unit, h_up, None), h_up, None, side)
            return
        for unit in extra[part]:
            arrived(unit, 1, h_down, None)
            send(unit, 5, region(unit, h_down, 0), h_down, 0, above)
            send(unit, 3, region(unit, h_down, None), h_down, None, side)
            arrived(unit, 2, h_up, None)
            send(unit, 6, region(unit, h_up, 1), h_up, 1, below)
            send(unit, 4, region(unit, h_up, None), h_up, None, side)

    def finish(part):
        if part == parts - 1:
            for unit in extra[part]:
                arrived(unit, 5, h_far, None)
                send(unit, 7, region(unit, h_far, None), h_far, None, side)
            return
        for unit in extra[part]:
            arrived(unit, 5, h_far, 0)
            send(unit, 7, region(unit, h_far, 0), h_far, 0, side)
            arrived(unit, 6, h_far, 1)
            send(unit, 8, region(unit, h_far, 1), h_far, 1, side)

    heads = 16
    queries = nope_vm.shape[0]
    row_head = lax.rem(lax.broadcasted_iota(jnp.int32, (queries, 1), 0), heads)
    row_request = lax.rem(lax.broadcasted_iota(jnp.int32, (queries, 1), 0) // heads, 8)
    get_nope.wait()
    get_absorb.wait()
    width = lat_vm.shape[2]

    def absorb(n, total):
        part_query = [
            jnp.where(row_head == ABSORB * n + h, nope_vm[...], jnp.zeros((), jnp.bfloat16))
            for h in range(ABSORB)
        ]
        weights = absorb_vm[pl.ds(ABSORB * n, ABSORB)].reshape(ABSORB * TILE, width)
        return total + jnp.dot(
            jnp.concatenate(part_query, axis=1), weights, preferred_element_type=jnp.float32
        )

    absorbed = lax.fori_loop(
        0, heads // ABSORB, absorb, jnp.zeros((queries, width), jnp.float32)
    )
    query[...] = absorbed.astype(jnp.bfloat16)
    get_qrope.wait()
    get_lat.wait()
    scale = 192.0**-0.5
    pair = 2 * TILE
    lane_row = lax.broadcasted_iota(jnp.int32, (1, TILE), 1)

    def score(i, peak):
        block = lat_vm[pl.ds(2 * i, 2)].reshape(pair, width)
        raw = lax.dot_general(
            query[...], block, (((1,), (1,)), ((), ())), preferred_element_type=jnp.float32
        )
        turned = []
        holders = []
        for b in range(2):
            turned.append(
                jnp.dot(qrope_vm[...], rope_vm[2 * i + b], preferred_element_type=jnp.float32)
            )
            g = lax.rem(me, per_row) * slots + 2 * i + b
            owner = owner_sm[me // per_row, g]
            left = length_sm[jnp.maximum(owner, 0)] - index_sm[me // per_row, g] * TILE
            holders.append(jnp.where(lane_row < left, owner, NEG))
        raw = (raw + jnp.concatenate(turned, axis=1)) * scale
        raw = jnp.where(jnp.concatenate(holders, axis=1) == row_request, raw, HIDDEN)
        scores[i] = raw
        return jnp.maximum(peak, raw)

    peak = lax.fori_loop(
        0, slots // 2, score, jnp.full((queries, pair), FLOOR, jnp.float32), unroll=UNROLL
    )
    peak = jnp.max(peak, axis=1, keepdims=True)

    def weigh(i, carry):
        total, summed = carry
        weights = jnp.exp(scores[i] - peak)
        block = lat_vm[pl.ds(2 * i, 2)].reshape(pair, width)
        summed = summed + jnp.dot(
            weights.astype(jnp.bfloat16), block, preferred_element_type=jnp.float32
        )
        return total + weights, summed

    total, summed = lax.fori_loop(
        0,
        slots // 2,
        weigh,
        (jnp.zeros((queries, pair), jnp.float32), jnp.zeros((queries, width), jnp.float32)),
        unroll=UNROLL,
    )
    total = jnp.sum(total, axis=1, keepdims=True)
    query[...] = summed.astype(jnp.bfloat16)
    get_value.wait()

    def project(n, result):
        both = jnp.concatenate([value_vm[2 * n], value_vm[2 * n + 1]], axis=1)
        got = jnp.dot(query[...], both, preferred_element_type=jnp.float32)
        result = jnp.where(row_head == 2 * n, got[:, :TILE], result)
        return jnp.where(row_head == 2 * n + 1, got[:, TILE:], result)

    projected = lax.fori_loop(
        0, heads // 2, project, jnp.zeros((queries, TILE), jnp.float32), unroll=UNROLL
    )
    wide = lax.broadcasted_iota(jnp.int32, (queries, TILE), 1)
    stats = jnp.where(
        wide < TILE // 2,
        jnp.broadcast_to(peak, (queries, TILE)),
        jnp.broadcast_to(total, (queries, TILE)),
    )
    x_send[:, 0] = projected.reshape(X, queries // X, TILE)
    x_send[:, 1] = stats.reshape(X, queries // X, TILE)
    x_got[x] = x_send[x]
    for k in range(1, X):
        peer = lax.rem(x + k, X)
        ship_part(x_send.at[peer], x_got.at[x], 0, z * X + peer)
    def first():
        wait_all(x_got, att_sem.at[0, 1])
        top, sums, totals = merge(x_got[...])
        z_send[:, 0] = sums.reshape(Z, 8, TILE)
        z_send[:, 1] = jnp.where(wide[: queries // X] < TILE // 2, top, totals).reshape(Z, 8, TILE)
        z_got[z] = z_send[z]
        for k in range(1, Z):
            peer = lax.rem(z + k, Z)
            ship_part(z_send.at[peer], z_got.at[z], 1, peer * X + x)

    def second():
        wait_all(z_got, att_sem.at[1, 1])
        top, sums, totals = merge(z_got[...])
        z_all[z] = sums / totals
        for k in range(1, Z):
            ship_part(z_all.at[z], z_all.at[z], 2, lax.rem(z + k, Z) * X + x)

    def third():
        wait_all(z_all, att_sem.at[2, 1])
        x_all[x] = z_all[...].reshape(queries // X, TILE)
        for k in range(1, X):
            ship_part(x_all.at[x], x_all.at[x], 3, z * X + lax.rem(x + k, X))

    place(0)
    first()
    place(1)
    relay(0)
    relay(1)
    place(2)
    finish(0)
    second()
    relay(2)
    place(3)
    finish(1)
    finish(2)
    third()
    relay(3)
    finish(3)
    wait_all(x_all, att_sem.at[3, 1])
    out_att[...] = x_all[...].reshape(queries, TILE)

    for unit in units:
        arrived(unit, 0, y * 2 + other, None)
        arrived(unit, 3, o_down, None)
        arrived(unit, 4, o_up, None)
        if unit in extra[parts - 1]:
            arrived(unit, 7, o_far, None)
        else:
            arrived(unit, 7, o_far, 0)
            arrived(unit, 8, o_far, 1)
    for copy in started:
        copy.wait_send()
    for part in range(parts):
        wait_all(sends[part], a2a_send.at[part])
    wait_all(x_send, att_sem.at[0, 0])
    wait_all(z_send, att_sem.at[1, 0])
    wait_all(z_all, att_sem.at[2, 0])
    wait_all(x_all, att_sem.at[3, 0])


def hand_out(att, lat, rope, out_att, out_lat, out_rope, turned, sem):
    step = lat.shape[0] // PIECES
    copies = []
    for n in range(PIECES):
        span = pl.ds(n * step, step)
        copies.append(pltpu.make_async_copy(lat.at[span], out_lat.at[span], sem.at[3 + n]))
        copies[-1].start()
    second = pltpu.make_async_copy(att, out_att, sem.at[1])
    second.start()

    def turn(p, carry):
        for n in range(rope.shape[0] // 2):
            low = rope[2 * n, p].astype(jnp.float32)
            high = rope[2 * n + 1, p].astype(jnp.float32)
            for b in range(2):
                span = slice(8 * b, 8 * b + 8)
                both = jnp.concatenate([low[span], high[span]], axis=0)
                turned[2 * p + b, ROWS * n : ROWS * (n + 1), :] = both.astype(jnp.bfloat16)
        return carry

    lax.fori_loop(0, rope.shape[1], turn, 0, unroll=2)
    third = pltpu.make_async_copy(turned, out_rope, sem.at[2])
    third.start()
    for copy in copies:
        copy.wait()
    second.wait()
    third.wait()


def shards(
    latent_cache,
    rope_cache,
    query_nope,
    query_rope,
    key_absorb,
    value_up_weight,
    block_request,
    block_index,
    request_length,
    move_plan,
):
    slots, block, width = latent_cache.shape
    rope_width = rope_cache.shape[2]
    steps, requests, heads, nope_width = query_nope.shape
    queries = steps * requests * heads
    insts = lax.axis_size("inst")
    heads_axis = lax.axis_size("head")
    bf16, f32, i32 = jnp.bfloat16, jnp.float32, jnp.int32
    tiles = [
        2 * len(LANE_TILES[p]) + (1 if p == ROPE_CHUNK else 0) for p in range(len(LANE_TILES))
    ]
    units = len(LANE_TILES) + 1
    anywhere = pl.BlockSpec(memory_space=pl.ANY)
    attention, moved, rope = pl.pallas_call(
        kernel,
        out_shape=(
            pltpu.VMEM((queries, TILE), f32),
            pltpu.VMEM(latent_cache.shape, bf16),
            pltpu.VMEM((heads_axis, slots // 2, ROWS, TILE), bf16),
        ),
        in_specs=[pl.BlockSpec(memory_space=pltpu.HBM)] * 10,
        out_specs=(pl.BlockSpec(memory_space=pltpu.VMEM),) * 3,
        scratch_shapes=[
            pltpu.VMEM((slots, block, width), bf16),
            pltpu.VMEM((slots, rope_width, block), bf16),
            pltpu.VMEM((queries, nope_width), bf16),
            pltpu.VMEM((queries, rope_width), bf16),
            pltpu.VMEM(key_absorb.shape, bf16),
            pltpu.VMEM(value_up_weight.shape, bf16),
            pltpu.VMEM((8, TILE), i32),
            pltpu.SMEM((8, TILE), i32),
            pltpu.SMEM((8, TILE), i32),
            pltpu.SMEM((8,), i32),
            pltpu.VMEM((slots, TILE), i32),
            pltpu.SMEM((slots, TILE), i32),
            pltpu.VMEM((slots, ROWS, width), bf16),
            pltpu.VMEM((slots, 8, TILE), f32),
            pltpu.VMEM((slots, 8, TILE), f32),
            pltpu.VMEM((queries, width), bf16),
            pltpu.VMEM((slots // 2, queries, 2 * TILE), f32),
            pltpu.VMEM((X, 2, queries // X, TILE), f32),
            pltpu.VMEM((X, 2, queries // X, TILE), f32),
            pltpu.VMEM((Z, 2, 8, TILE), f32),
            pltpu.VMEM((Z, 2, 8, TILE), f32),
            pltpu.VMEM((Z, 8, TILE), f32),
            pltpu.VMEM((X, queries // X, TILE), f32),
        ]
        + [pltpu.VMEM((insts, n, ROWS, TILE), bf16) for n in tiles]
        + [pltpu.VMEM((insts, n, ROWS, TILE), bf16) for n in tiles]
        + [
            pltpu.SemaphoreType.DMA((12,)),
            pltpu.SemaphoreType.DMA((len(tiles),)),
            pltpu.SemaphoreType.DMA((len(tiles),)),
            pltpu.SemaphoreType.DMA((4, 2)),
            pltpu.SemaphoreType.DMA((units, 9)),
            pltpu.SemaphoreType.DMA((units, 9)),
        ],
        compiler_params=pltpu.CompilerParams(
            collective_id=0, has_side_effects=True, vmem_limit_bytes=40 * 2**20
        ),
        name="decode_and_move",
    )(
        *(
            pltpu.with_memory_space_constraint(a, pltpu.HBM)
            for a in (
                latent_cache,
                rope_cache.swapaxes(1, 2),
                query_nope.reshape(queries, nope_width),
                query_rope.reshape(queries, rope_width),
                key_absorb,
                value_up_weight,
                block_request.reshape(8, TILE),
                block_index.reshape(8, TILE),
                request_length,
                move_plan.reshape(8, TILE),
            )
        )
    )
    inside = [pltpu.with_memory_space_constraint(a, pltpu.VMEM) for a in (attention, moved, rope)]
    attention, moved, rope = pl.pallas_call(
        hand_out,
        out_shape=(
            jax.ShapeDtypeStruct((queries, TILE), f32),
            jax.ShapeDtypeStruct(latent_cache.shape, bf16),
            jax.ShapeDtypeStruct((slots, rope_width, block), bf16),
        ),
        in_specs=[pl.BlockSpec(memory_space=pltpu.VMEM)] * 3,
        out_specs=(anywhere,) * 3,
        scratch_shapes=[
            pltpu.VMEM((slots, rope_width, block), bf16),
            pltpu.SemaphoreType.DMA((3 + PIECES,)),
        ],
        compiler_params=pltpu.CompilerParams(vmem_limit_bytes=16 * 2**20),
        name="hand_out",
    )(*inside)
    attention = attention.reshape(steps, requests, heads, TILE)
    return attention, moved, rope.swapaxes(1, 2)


def solution(mesh):
    return jax.shard_map(
        shards,
        mesh=mesh,
        in_specs=(
            P("inst", None, None),
            P("inst", None, None),
            P(None, None, "head", None),
            P(None, None, "head", None),
            P("head", None, None),
            P("head", None, None),
            P(),
            P(),
            P(),
            P(),
        ),
        out_specs=(P(None, None, "head", None), P("inst", None, None), P("inst", None, None)),
        check_vma=False,
    )
```

```python
import functools

import jax
import jax.numpy as jnp
from jax import lax
from jax.experimental import pallas as pl
from jax.experimental.pallas import tpu as pltpu
from jax.sharding import PartitionSpec as P

MESH = pl.DeviceIdType.MESH
HIDDEN = -1e30
FLOOR = -1e29
TILE = 128
ROWS = 16
LANE_TILES = ((0,),(1,),(2,),(3,))
ROPE_CHUNK = 0
WINDOW = 2
PIECES = 8
Z, X = 8, 4
ROW_ORDER = (0, 1, 2, 3, 7, 4, 5, 6)
NEG = -1
ABSORB = 8
UNROLL = 4


def kernel(
    lat_hbm,
    rope_hbm,
    nope_hbm,
    qrope_hbm,
    absorb_hbm,
    value_hbm,
    owner_hbm,
    index_hbm,
    length_hbm,
    plan_hbm,
    out_att,
    out_lat,
    out_rope,
    lat_vm,
    rope_vm,
    nope_vm,
    qrope_vm,
    absorb_vm,
    value_vm,
    plan_vm,
    owner_sm,
    index_sm,
    length_sm,
    table_vm,
    table_sm,
    share,
    rope_share,
    rope_got,
    query,
    scores,
    x_send,
    x_got,
    z_send,
    z_got,
    z_all,
    x_all,
    *rest,

):
    parts = len(LANE_TILES)
    sends, gots = rest[:parts], rest[parts : 2 * parts]
    in_sem, a2a_send, a2a_recv, att_sem, ag_send, ag_recv = rest[2 * parts :]
    insts = lax.axis_size("inst")
    me = lax.axis_index("inst")
    head = lax.axis_index("head")
    core = lax.rem(head, 2)
    y = head // 2
    up = lax.rem(y + 1, 4)
    down = lax.rem(y + 3, 4)
    far = lax.rem(y + 2, 4)
    other = 1 - core
    slots = lat_vm.shape[0]
    z, x = me // X, lax.rem(me, X)

    def fetch(k, source, target):
        copy = pltpu.make_async_copy(source, target, in_sem.at[k])
        copy.start()
        return copy

    rows = pl.ds(pl.multiple_of(head * ROWS, ROWS), ROWS)
    get_plan = fetch(0, plan_hbm, plan_vm)
    get_share = fetch(1, lat_hbm.at[:, rows, :], share)
    get_rope = fetch(2, rope_hbm, rope_vm)
    get_owner = fetch(3, owner_hbm, owner_sm)
    get_index = fetch(4, index_hbm, index_sm)
    get_length = fetch(5, length_hbm, length_sm)
    get_nope = fetch(6, nope_hbm, nope_vm)
    get_absorb = fetch(7, absorb_hbm, absorb_vm)
    get_qrope = fetch(8, qrope_hbm, qrope_vm)
    get_lat = fetch(9, lat_hbm, lat_vm)
    get_value = fetch(10, value_hbm, value_vm)

    barrier = pltpu.get_barrier_semaphore()

    def greet(k, carry):
        pl.semaphore_signal(
            barrier,
            inc=1,
            device_id={"inst": lax.rem(me + k, insts)},
            device_id_type=MESH,
        )
        return carry

    lax.fori_loop(1, insts, greet, 0)
    mates = (y * 2 + other, up * 2 + core, down * 2 + core, far * 2 + core)
    for mate in mates:
        pl.semaphore_signal(barrier, inc=1, device_id={"head": mate}, device_id_type=MESH)

    get_plan.wait()
    plan = plan_vm[...]
    lane = lax.broadcasted_iota(jnp.int32, (8, TILE), 1)
    row = lax.broadcasted_iota(jnp.int32, (8, TILE), 0)
    per_row = TILE // slots
    group = lane // slots
    within = lane - group * slots
    seen = jnp.where((plan >> 5) == me, 1, 0)
    for d in (1, 2, 4, 8, 16):
        seen = jnp.maximum(seen, jnp.where(within >= d, pltpu.roll(seen, d, 1), 0))
    rank = jnp.where(within >= 1, pltpu.roll(seen, 1, 1), 0)
    code = (row * per_row + group) * 2 + rank
    column = lax.broadcasted_iota(jnp.int32, (slots, TILE), 0)
    lanes = lax.broadcasted_iota(jnp.int32, (slots, TILE), 1)
    hit = jnp.full((slots, TILE), NEG, jnp.int32)
    for r in range(8):
        wanted = jnp.broadcast_to(plan[r : r + 1, :], (slots, TILE)) == me * slots + column
        hit = jnp.maximum(
            hit, jnp.where(wanted, jnp.broadcast_to(code[r : r + 1, :], (slots, TILE)), NEG)
        )
    land = jnp.max(hit, axis=1, keepdims=True)
    mine = plan_vm[pl.ds(me // per_row, 1), :]
    own_lane = lax.rem(me, per_row) * slots + column
    own = jnp.max(
        jnp.where(lanes == own_lane, jnp.broadcast_to(mine, (slots, TILE)), NEG),
        axis=1,
        keepdims=True,
    )
    mine = jnp.where(group[:1] == lax.rem(me, per_row), mine >> 5, NEG)
    goes = jnp.broadcast_to(mine, (slots, TILE)) == column
    place = lanes - lanes // slots * slots
    first = jnp.min(jnp.where(goes, place, slots), axis=1, keepdims=True)
    last = jnp.max(jnp.where(goes, place, 0), axis=1, keepdims=True)
    first = jnp.where(first >= slots, 0, first)
    table_vm[...] = jnp.where(
        lanes == 0,
        jnp.broadcast_to(first, (slots, TILE)),
        jnp.where(
            lanes == 1,
            jnp.broadcast_to(last, (slots, TILE)),
            jnp.where(
                lanes == 2,
                jnp.broadcast_to(land, (slots, TILE)),
                jnp.broadcast_to(own, (slots, TILE)),
            ),
        ),
    )
    get_table = fetch(11, table_vm, table_sm)

    get_rope.wait()
    half = pl.ds(pl.multiple_of(y * ROWS, ROWS), ROWS)

    def cut_rope(t, carry):
        piece = rope_vm[t, half, :].astype(jnp.float32)
        rope_share[t] = jnp.where(core == 0, piece[:8], piece[8:])
        return carry

    lax.fori_loop(0, slots, cut_rope, 0, unroll=4)
    get_share.wait()
    get_table.wait()
    get_owner.wait()
    get_index.wait()
    get_length.wait()

    def dispatch(part):
        if part >= parts:
            return
        tiles = LANE_TILES[part]
        count = len(tiles)
        buffer = sends[part]

        def pack(j, carry):
            picks = (table_sm[j, 0], table_sm[j, 1])
            for seat in range(2):
                for n, tile in enumerate(tiles):
                    buffer[j, seat * count + n] = share[
                        picks[seat], :, tile * TILE : (tile + 1) * TILE
                    ]
            if part == ROPE_CHUNK:
                buffer[j, 2 * count] = jnp.concatenate(
                    [rope_share[picks[0]], rope_share[picks[1]]], axis=0
                ).astype(jnp.bfloat16)
            return carry

        lax.fori_loop(0, insts, pack, 0, unroll=8)
        if part == 0:
            pl.semaphore_wait(barrier, insts - 1 + len(mates))

        def ship(k, carry):
            peer = carry * X + lax.rem(x + k, X)

            @pl.when(peer != me)
            def _():
                pltpu.make_async_remote_copy(
                    src_ref=buffer.at[peer],
                    dst_ref=gots[part].at[me],
                    send_sem=a2a_send.at[part],
                    recv_sem=a2a_recv.at[part],
                    device_id={"inst": peer},
                    device_id_type=MESH,
                ).start()

            return carry

        for row in ROW_ORDER:
            lax.fori_loop(0, X, ship, row)

    for part in range(min(WINDOW, parts)):
        dispatch(part)

    def wait_all(buffer, sem):
        whole = buffer.at[pl.ds(0, buffer.shape[0] - 1)]
        pltpu.make_async_copy(whole, whole, sem).wait()

    def ship_part(source, target, k, peer):
        pltpu.make_async_remote_copy(
            src_ref=source,
            dst_ref=target,
            send_sem=att_sem.at[k, 0],
            recv_sem=att_sem.at[k, 1],
            device_id={"inst": peer},
            device_id_type=MESH,
        ).start()

    def merge(got):
        partial, stat = got[:, 0], got[:, 1]
        peaks, totals = stat[:, :, :1], stat[:, :, TILE // 2 : TILE // 2 + 1]
        top = jnp.max(peaks, axis=0, keepdims=True)
        weight = jnp.exp(peaks - top)
        return top[0], jnp.sum(partial * weight, axis=0), jnp.sum(totals * weight, axis=0)

    def region(unit, h, which):
        n = slots if unit < parts else slots // 2
        span = {
            None: pl.ds(0, n),
            0: pl.ds(0, n // 2),
            1: pl.ds(n // 2, n // 2),
        }[which]
        if unit < parts:
            tiles = LANE_TILES[unit]
            return out_lat.at[
                span,
                pl.ds(pl.multiple_of(h * ROWS, ROWS), ROWS),
                pl.ds(tiles[0] * TILE, len(tiles) * TILE),
            ]
        return out_rope.at[h, span]

    started = []

    def send(unit, k, source, h, which, mate):
        copy = pltpu.make_async_remote_copy(
            src_ref=source,
            dst_ref=region(unit, h, which),
            send_sem=ag_send.at[unit, k],
            recv_sem=ag_recv.at[unit, k],
            device_id={"head": mate},
            device_id_type=MESH,
        )
        copy.start()
        started.append(copy)

    def arrived(unit, k, h, which):
        here = region(unit, h, which)
        pltpu.make_async_copy(here, here, ag_recv.at[unit, k]).wait()

    side, above, below, _ = mates
    h_up, h_down, h_far = up * 2 + core, down * 2 + core, far * 2 + core
    o_up, o_down, o_far = up * 2 + other, down * 2 + other, far * 2 + other
    extra = {p: [p] * (len(LANE_TILES[p]) > 0) + [parts] * (p == ROPE_CHUNK) for p in range(parts)}
    units = [unit for p in range(parts) for unit in extra[p]]

    def place(part):
        tiles = LANE_TILES[part]
        count = len(tiles)
        buffer = gots[part]
        wait_all(buffer, a2a_recv.at[part])
        dispatch(part + WINDOW)

        def put(t, carry):
            where = table_sm[t, 2]
            g = lax.rem(me, per_row) * slots + t
            keep = (owner_sm[me // per_row, g] >= 0) & (table_sm[t, 3] < 0)
            spot = jnp.maximum(where, 0)
            source, seat = spot // 2, lax.rem(spot, 2)
            for n, tile in enumerate(tiles):
                span = slice(tile * TILE, (tile + 1) * TILE)
                moved = buffer[source, seat * count + n]
                kept = share[t, :, span]
                zero = jnp.zeros_like(moved)
                out_lat[t, rows, span] = jnp.where(
                    keep, kept, jnp.where(where >= 0, moved, zero)
                )
            if part == ROPE_CHUNK:
                pieces = buffer[source, 2 * count].astype(jnp.float32)
                moved = jnp.where(seat == 0, pieces[:8], pieces[8:])
                zero = jnp.zeros_like(moved)
                rope_got[t] = jnp.where(
                    keep, rope_share[t], jnp.where(where >= 0, moved, zero)
                )
            return carry

        lax.fori_loop(0, slots, put, 0, unroll=16)
        if part == ROPE_CHUNK:
            out_rope[head] = rope_got[...].reshape(slots // 2, ROWS, TILE).astype(jnp.bfloat16)
        for unit in extra[part]:
            source = region(unit, head, None)
            if part == parts - 1:
                send(unit, 5, source, head, None, far * 2 + core)
            send(unit, 1, source, head, None, above)
            send(unit, 2, source, head, None, below)
            send(unit, 0, source, head, None, side)

    def relay(part):
        if part == parts - 1:
            for unit in extra[part]:
                arrived(unit, 1, h_down, None)
                send(unit, 3, region(unit, h_down, None), h_down, None, side)
                arrived(unit, 2, h_up, None)
                send(unit, 4, region(unit, h_up, None), h_up, None, side)
            return
        for unit in extra[part]:
            arrived(unit, 1, h_down, None)
            send(unit, 5, region(unit, h_down, 0), h_down, 0, above)
            send(unit, 3, region(unit, h_down, None), h_down, None, side)
            arrived(unit, 2, h_up, None)
            send(unit, 6, region(unit, h_up, 1), h_up, 1, below)
            send(unit, 4, region(unit, h_up, None), h_up, None, side)

    def finish(part):
        if part == parts - 1:
            for unit in extra[part]:
                arrived(unit, 5, h_far, None)
                send(unit, 7, region(unit, h_far, None), h_far, None, side)
            return
        for unit in extra[part]:
            arrived(unit, 5, h_far, 0)
            send(unit, 7, region(unit, h_far, 0), h_far, 0, side)
            arrived(unit, 6, h_far, 1)
            send(unit, 8, region(unit, h_far, 1), h_far, 1, side)

    heads = 16
    queries = nope_vm.shape[0]
    row_head = lax.rem(lax.broadcasted_iota(jnp.int32, (queries, 1), 0), heads)
    row_request = lax.rem(lax.broadcasted_iota(jnp.int32, (queries, 1), 0) // heads, 8)
    get_nope.wait()
    get_absorb.wait()
    width = lat_vm.shape[2]

    def absorb(n, total):
        part_query = [
            jnp.where(row_head == ABSORB * n + h, nope_vm[...], jnp.zeros((), jnp.bfloat16))
            for h in range(ABSORB)
        ]
        weights = absorb_vm[pl.ds(ABSORB * n, ABSORB)].reshape(ABSORB * TILE, width)
        return total + jnp.dot(
            jnp.concatenate(part_query, axis=1), weights, preferred_element_type=jnp.float32
        )

    absorbed = lax.fori_loop(
        0, heads // ABSORB, absorb, jnp.zeros((queries, width), jnp.float32)
    )
    query[...] = absorbed.astype(jnp.bfloat16)
    get_qrope.wait()
    get_lat.wait()
    scale = 192.0**-0.5
    pair = 2 * TILE
    lane_row = lax.broadcasted_iota(jnp.int32, (1, TILE), 1)

    def score(i, peak):
        block = lat_vm[pl.ds(2 * i, 2)].reshape(pair, width)
        raw = lax.dot_general(
            query[...], block, (((1,), (1,)), ((), ())), preferred_element_type=jnp.float32
        )
        turned = []
        holders = []
        for b in range(2):
            turned.append(
                jnp.dot(qrope_vm[...], rope_vm[2 * i + b], preferred_element_type=jnp.float32)
            )
            g = lax.rem(me, per_row) * slots + 2 * i + b
            owner = owner_sm[me // per_row, g]
            left = length_sm[jnp.maximum(owner, 0)] - index_sm[me // per_row, g] * TILE
            holders.append(jnp.where(lane_row < left, owner, NEG))
        raw = (raw + jnp.concatenate(turned, axis=1)) * scale
        raw = jnp.where(jnp.concatenate(holders, axis=1) == row_request, raw, HIDDEN)
        scores[i] = raw
        return jnp.maximum(peak, raw)

    peak = lax.fori_loop(
        0, slots // 2, score, jnp.full((queries, pair), FLOOR, jnp.float32), unroll=UNROLL
    )
    peak = jnp.max(peak, axis=1, keepdims=True)

    def weigh(i, carry):
        total, summed = carry
        weights = jnp.exp(scores[i] - peak)
        block = lat_vm[pl.ds(2 * i, 2)].reshape(pair, width)
        summed = summed + jnp.dot(
            weights.astype(jnp.bfloat16), block, preferred_element_type=jnp.float32
        )
        return total + weights, summed

    total, summed = lax.fori_loop(
        0,
        slots // 2,
        weigh,
        (jnp.zeros((queries, pair), jnp.float32), jnp.zeros((queries, width), jnp.float32)),
        unroll=UNROLL,
    )
    total = jnp.sum(total, axis=1, keepdims=True)
    query[...] = summed.astype(jnp.bfloat16)
    get_value.wait()

    def project(n, result):
        both = jnp.concatenate([value_vm[2 * n], value_vm[2 * n + 1]], axis=1)
        got = jnp.dot(query[...], both, preferred_element_type=jnp.float32)
        result = jnp.where(row_head == 2 * n, got[:, :TILE], result)
        return jnp.where(row_head == 2 * n + 1, got[:, TILE:], result)

    projected = lax.fori_loop(
        0, heads // 2, project, jnp.zeros((queries, TILE), jnp.float32), unroll=UNROLL
    )
    wide = lax.broadcasted_iota(jnp.int32, (queries, TILE), 1)
    stats = jnp.where(
        wide < TILE // 2,
        jnp.broadcast_to(peak, (queries, TILE)),
        jnp.broadcast_to(total, (queries, TILE)),
    )
    x_send[:, 0] = projected.reshape(X, queries // X, TILE)
    x_send[:, 1] = stats.reshape(X, queries // X, TILE)
    x_got[x] = x_send[x]
    for k in range(1, X):
        peer = lax.rem(x + k, X)
        ship_part(x_send.at[peer], x_got.at[x], 0, z * X + peer)
    def first():
        wait_all(x_got, att_sem.at[0, 1])
        top, sums, totals = merge(x_got[...])
        z_send[:, 0] = sums.reshape(Z, 8, TILE)
        z_send[:, 1] = jnp.where(wide[: queries // X] < TILE // 2, top, totals).reshape(Z, 8, TILE)
        z_got[z] = z_send[z]
        for k in range(1, Z):
            peer = lax.rem(z + k, Z)
            ship_part(z_send.at[peer], z_got.at[z], 1, peer * X + x)

    def second():
        wait_all(z_got, att_sem.at[1, 1])
        top, sums, totals = merge(z_got[...])
        z_all[z] = sums / totals
        for k in range(1, Z):
            ship_part(z_all.at[z], z_all.at[z], 2, lax.rem(z + k, Z) * X + x)

    def third():
        wait_all(z_all, att_sem.at[2, 1])
        x_all[x] = z_all[...].reshape(queries // X, TILE)
        for k in range(1, X):
            ship_part(x_all.at[x], x_all.at[x], 3, z * X + lax.rem(x + k, X))

    place(0)
    first()
    place(1)
    relay(0)
    relay(1)
    place(2)
    finish(0)
    second()
    relay(2)
    place(3)
    finish(1)
    finish(2)
    third()
    relay(3)
    finish(3)
    wait_all(x_all, att_sem.at[3, 1])
    out_att[...] = x_all[...].reshape(queries, TILE)

    for unit in units:
        arrived(unit, 0, y * 2 + other, None)
        arrived(unit, 3, o_down, None)
        arrived(unit, 4, o_up, None)
        if unit in extra[parts - 1]:
            arrived(unit, 7, o_far, None)
        else:
            arrived(unit, 7, o_far, 0)
            arrived(unit, 8, o_far, 1)
    for copy in started:
        copy.wait_send()
    for part in range(parts):
        wait_all(sends[part], a2a_send.at[part])
    wait_all(x_send, att_sem.at[0, 0])
    wait_all(z_send, att_sem.at[1, 0])
    wait_all(z_all, att_sem.at[2, 0])
    wait_all(x_all, att_sem.at[3, 0])


def hand_out(att, lat, rope, out_att, out_lat, out_rope, turned, sem):
    step = lat.shape[0] // PIECES
    copies = []
    for n in range(PIECES):
        span = pl.ds(n * step, step)
        copies.append(pltpu.make_async_copy(lat.at[span], out_lat.at[span], sem.at[3 + n]))
        copies[-1].start()
    second = pltpu.make_async_copy(att, out_att, sem.at[1])
    second.start()

    def turn(p, carry):
        for n in range(rope.shape[0] // 2):
            low = rope[2 * n, p].astype(jnp.float32)
            high = rope[2 * n + 1, p].astype(jnp.float32)
            for b in range(2):
                span = slice(8 * b, 8 * b + 8)
                both = jnp.concatenate([low[span], high[span]], axis=0)
                turned[2 * p + b, ROWS * n : ROWS * (n + 1), :] = both.astype(jnp.bfloat16)
        return carry

    lax.fori_loop(0, rope.shape[1], turn, 0, unroll=2)
    third = pltpu.make_async_copy(turned, out_rope, sem.at[2])
    third.start()
    for copy in copies:
        copy.wait()
    second.wait()
    third.wait()


def shards(
    latent_cache,
    rope_cache,
    query_nope,
    query_rope,
    key_absorb,
    value_up_weight,
    block_request,
    block_index,
    request_length,
    move_plan,
):
    slots, block, width = latent_cache.shape
    rope_width = rope_cache.shape[2]
    steps, requests, heads, nope_width = query_nope.shape
    queries = steps * requests * heads
    insts = lax.axis_size("inst")
    heads_axis = lax.axis_size("head")
    bf16, f32, i32 = jnp.bfloat16, jnp.float32, jnp.int32
    tiles = [
        2 * len(LANE_TILES[p]) + (1 if p == ROPE_CHUNK else 0) for p in range(len(LANE_TILES))
    ]
    units = len(LANE_TILES) + 1
    anywhere = pl.BlockSpec(memory_space=pl.ANY)
    attention, moved, rope = pl.pallas_call(
        kernel,
        out_shape=(
            pltpu.VMEM((queries, TILE), f32),
            pltpu.VMEM(latent_cache.shape, bf16),
            pltpu.VMEM((heads_axis, slots // 2, ROWS, TILE), bf16),
        ),
        in_specs=[pl.BlockSpec(memory_space=pltpu.HBM)] * 10,
        out_specs=(pl.BlockSpec(memory_space=pltpu.VMEM),) * 3,
        scratch_shapes=[
            pltpu.VMEM((slots, block, width), bf16),
            pltpu.VMEM((slots, rope_width, block), bf16),
            pltpu.VMEM((queries, nope_width), bf16),
            pltpu.VMEM((queries, rope_width), bf16),
            pltpu.VMEM(key_absorb.shape, bf16),
            pltpu.VMEM(value_up_weight.shape, bf16),
            pltpu.VMEM((8, TILE), i32),
            pltpu.SMEM((8, TILE), i32),
            pltpu.SMEM((8, TILE), i32),
            pltpu.SMEM((8,), i32),
            pltpu.VMEM((slots, TILE), i32),
            pltpu.SMEM((slots, TILE), i32),
            pltpu.VMEM((slots, ROWS, width), bf16),
            pltpu.VMEM((slots, 8, TILE), f32),
            pltpu.VMEM((slots, 8, TILE), f32),
            pltpu.VMEM((queries, width), bf16),
            pltpu.VMEM((slots // 2, queries, 2 * TILE), f32),
            pltpu.VMEM((X, 2, queries // X, TILE), f32),
            pltpu.VMEM((X, 2, queries // X, TILE), f32),
            pltpu.VMEM((Z, 2, 8, TILE), f32),
            pltpu.VMEM((Z, 2, 8, TILE), f32),
            pltpu.VMEM((Z, 8, TILE), f32),
            pltpu.VMEM((X, queries // X, TILE), f32),
        ]
        + [pltpu.VMEM((insts, n, ROWS, TILE), bf16) for n in tiles]
        + [pltpu.VMEM((insts, n, ROWS, TILE), bf16) for n in tiles]
        + [
            pltpu.SemaphoreType.DMA((12,)),
            pltpu.SemaphoreType.DMA((len(tiles),)),
            pltpu.SemaphoreType.DMA((len(tiles),)),
            pltpu.SemaphoreType.DMA((4, 2)),
            pltpu.SemaphoreType.DMA((units, 9)),
            pltpu.SemaphoreType.DMA((units, 9)),
        ],
        compiler_params=pltpu.CompilerParams(
            collective_id=0, has_side_effects=True, vmem_limit_bytes=40 * 2**20
        ),
        name="decode_and_move",
    )(
        *(
            pltpu.with_memory_space_constraint(a, pltpu.HBM)
            for a in (
                latent_cache,
                rope_cache.swapaxes(1, 2),
                query_nope.reshape(queries, nope_width),
                query_rope.reshape(queries, rope_width),
                key_absorb,
                value_up_weight,
                block_request.reshape(8, TILE),
                block_index.reshape(8, TILE),
                request_length,
                move_plan.reshape(8, TILE),
            )
        )
    )
    inside = [pltpu.with_memory_space_constraint(a, pltpu.VMEM) for a in (attention, moved, rope)]
    attention, moved, rope = pl.pallas_call(
        hand_out,
        out_shape=(
            jax.ShapeDtypeStruct((queries, TILE), f32),
            jax.ShapeDtypeStruct(latent_cache.shape, bf16),
            jax.ShapeDtypeStruct((slots, rope_width, block), bf16),
        ),
        in_specs=[pl.BlockSpec(memory_space=pltpu.VMEM)] * 3,
        out_specs=(anywhere,) * 3,
        scratch_shapes=[
            pltpu.VMEM((slots, rope_width, block), bf16),
            pltpu.SemaphoreType.DMA((3 + PIECES,)),
        ],
        compiler_params=pltpu.CompilerParams(vmem_limit_bytes=16 * 2**20),
        name="hand_out",
    )(*inside)
    attention = attention.reshape(steps, requests, heads, TILE)
    return attention, moved, rope.swapaxes(1, 2)


def solution(mesh):
    return jax.shard_map(
        shards,
        mesh=mesh,
        in_specs=(
            P("inst", None, None),
            P("inst", None, None),
            P(None, None, "head", None),
            P(None, None, "head", None),
            P("head", None, None),
            P("head", None, None),
            P(),
            P(),
            P(),
            P(),
        ),
        out_specs=(P(None, None, "head", None), P("inst", None, None), P("inst", None, None)),
        check_vma=False,
    )
```
